128 devices in a mesh: row: 8 (over x, y_lo), col: 16 (over z, y_hi, core).
Axes of the slice: x: 4, y: 4 (y_hi: 2, y_lo: 2; y = y_hi * 2 + y_lo), z: 4, core: 2. Of those that a mesh axis runs over, the one named last changes fastest.
Arguments:
- right_side: float32 [1024, 128], P('row'), may hold values from -6 to 6
- factor_window: float32 [1024, 1024], P('row', 'col'), may hold values from -0.125 to 0.125
- diag_inverse: float32 [1024, 128], P('row'), as said below
- phase_cov: bfloat16 [1024, 65536], P('col', 'row'), may hold values from -0.1875 to 0.1875
Outputs:
- basis: float32 [128, 512, 128], P('row', 'col')
- solved: float32 [1024, 128], P('col')
The draws below stay inside these ranges and needn't reach their ends.
Inputs may be any that keep to these rules, and one draw needn't show every extreme that they name: `diag_inverse`: each block of 128 rows is a lower triangular matrix with a diagonal between 0.5 and 2.
All inputs are finite; a program needn't handle non-finite values.
Results may differ from the reference program's by a relative error of at most 0.0043.
Values sent between devices are 32-bit elements; how exact they have to be, the bound alone decides.
No kernel may reach another device: no remote copies, remote signals or barrier semaphores. Data moves between devices by JAX's collectives and lax.ppermute only.
A program may use at most 64 MiB of HBM per device.

```python
import jax
import jax.numpy as jnp
from jax import lax

ROWS_DEV = 128
RANK = 128
TILE_ROWS = 512
K = 1024
TILES_ALL = 128
PHASE = 65536
N_ROW = 8


def draw_diag_inverse(key, part):
    first, second = jax.random.split(jax.random.fold_in(key, 7), 2)
    diagonal = jax.random.uniform(first, (K,), jnp.float32, 0.5, 2.0)
    offdiag = 0.5 * jax.random.normal(second, (K, ROWS_DEV), jnp.float32) / jnp.sqrt(jnp.float32(ROWS_DEV))
    local_row = (jnp.arange(K) % ROWS_DEV)[:, None]
    columns = jnp.arange(ROWS_DEV)[None, :]
    return jnp.where(columns < local_row, offdiag, 0.0) + jnp.where(columns == local_row, diagonal[:, None], 0.0)


def levels(stream_key, dims, cuts, smallest, high):
    def one(dim, shards_of):
        steps = jax.random.uniform(jax.random.fold_in(jax.random.fold_in(stream_key, 6), dim), (shards_of,), jnp.float32, smallest / len(cuts), high / len(cuts))
        return jnp.repeat(jnp.exp(steps), dims[dim] // shards_of).reshape((-1,) + (1,) * (len(dims) - dim - 1))

    gain = one(*cuts[0])
    for cut in cuts[1:]:
        gain = gain * one(*cut)
    return gain


def scatter_about(own_key, shape, scale, most, cuts=(), held_as=jnp.bfloat16):
    result = scale * jax.random.normal(own_key, shape, jnp.float32)
    if cuts:
        result = result * levels(own_key, shape, cuts, -0.22, 0.18)
    return jnp.clip(result, -most, most).astype(held_as)


def setup_inputs(seed: int = 0) -> dict:
    streams_of = jax.random.split(jax.random.key(seed), 5)
    right_side = scatter_about(streams_of[0], (K, RANK), 1.0, 6.0, ((0, 8),), jnp.float32)
    factor_window = scatter_about(streams_of[1], (K, K), (2 * K) ** -0.5, 0.125, ((0, 8), (1, 16)), jnp.float32)
    diag_inverse = draw_diag_inverse(jax.random.fold_in(streams_of[4], 71), 0)
    phase_cov = scatter_about(streams_of[3], (K, PHASE), K ** -0.5, 0.1875, ((0, 16), (1, 8)))
    return {"right_side": right_side, "factor_window": factor_window, "diag_inverse": diag_inverse, "phase_cov": phase_cov}


def tile_basis(lower, tile):
    return jax.scipy.linalg.solve_triangular(lower, tile.T, lower=True).T

def reference(right_side, factor_window, diag_inverse, phase_cov):
    pieces = []
    for block_index in range(N_ROW):
        start_row = block_index * ROWS_DEV
        remaining = right_side[start_row:start_row + ROWS_DEV]
        if block_index > 0:
            earlier = jnp.concatenate(pieces, axis=0)
            remaining = remaining - jnp.dot(factor_window[start_row:start_row + ROWS_DEV, :start_row].astype(jnp.float32), earlier.astype(jnp.float32), precision=lax.Precision.HIGHEST, preferred_element_type=jnp.float32)
        pieces.append(jnp.dot(diag_inverse[start_row:start_row + ROWS_DEV].astype(jnp.float32), remaining.astype(jnp.float32), precision=lax.Precision.HIGHEST, preferred_element_type=jnp.float32))
    solved = jnp.concatenate(pieces, axis=0)
    solved_low = solved.astype(jnp.bfloat16)
    weighted = jnp.dot(phase_cov.T.astype(jnp.float32), solved_low.astype(jnp.float32), preferred_element_type=jnp.float32)
    tiles = weighted.reshape(TILES_ALL, TILE_ROWS, RANK)
    gram = jnp.einsum('tsr,tsq->trq', tiles, tiles, precision=lax.Precision.HIGHEST)
    lower = jnp.linalg.cholesky(gram)
    basis = jax.vmap(tile_basis)(lower, tiles)
    return (basis, solved)
```

```python
import functools

import jax
import jax.numpy as jnp
from jax import lax
from jax.experimental import pallas as pl
from jax.experimental.pallas import tpu as pltpu
from jax.sharding import PartitionSpec as P

TILE_ROWS = 512
PANEL = 32
HIGHEST = lax.Precision.HIGHEST
VMEM_BYTES = 48 * 1024 * 1024


def contract(a, b, da, db):
    return lax.dot_general(a, b, (((da,), (db,)), ((), ())), precision=HIGHEST, preferred_element_type=jnp.float32)


def split(a):
    high = a.astype(jnp.bfloat16)
    return high, (a - high.astype(jnp.float32)).astype(jnp.bfloat16)


def dot3(a, b):
    dot = functools.partial(jnp.dot, preferred_element_type=jnp.float32)
    return dot(a[0], b[0]) + (dot(a[0], b[1]) + dot(a[1], b[0]))


def prepare(col_ref, right_ref, factor_ref, diag_ref, out_ref, scratch):
    diag = diag_ref[...]
    half = factor_ref.shape[1]
    chunk = out_ref.shape[0] - half
    out_ref[:half] = contract(factor_ref[...], diag, 0, 1)
    scratch[...] = contract(right_ref[...], diag, 0, 1)
    out_ref[half:] = scratch[pl.ds(pl.multiple_of(col_ref[0] * chunk, chunk), chunk), :]


def factor_and_invert(work, size):
    rows = lax.broadcasted_iota(jnp.int32, (PANEL, 1), 0)
    for start in range(0, size, PANEL):
        panel = work[start : start + PANEL, :]
        for k in range(PANEL):
            column = panel[:, start + k : start + k + 1]
            scale = lax.rsqrt(column[k : k + 1, :])
            row = panel[k : k + 1, :] * scale
            below = jnp.where(rows > k, column * scale, 0.0)
            panel = jnp.where(rows == k, row, panel - below * row)
        work[start : start + PANEL, :] = panel
        rest = start + PANEL
        if rest < size:
            work[rest:, :] -= contract(panel[:, rest:size], panel, 0, 0)


def finish(col_ref, pieces_ref, phase_ref, basis_ref, solved_ref, solved_t, work):
    blocks = solved_t.shape[0]
    size = solved_t.shape[1]
    quarter = size // 4
    current = []
    for i in range(blocks):
        parts = [pieces_ref[core, i * blocks + j, quarter:, :] for j in range(blocks) for core in range(2)]
        current.append(jnp.concatenate(parts, axis=0))
    for j in range(blocks):
        solved_t[j] = current[j]
        if j + 1 == blocks:
            break
        solved_pair = split(current[j])
        for i in range(j + 1, blocks):
            own, other = i * blocks + j, (blocks - 1 - i) * blocks + blocks - 1 - j
            factor = jnp.concatenate([pieces_ref[core, at, :quarter, :] for core in range(2) for at in (own, other)], axis=0)
            current[i] = current[i] - dot3(solved_pair, split(factor))
    col = col_ref[0]
    half = solved_ref.shape[0]
    work[:, :size] = solved_t[col // 2].T
    solved_ref[...] = work[pl.ds(pl.multiple_of(col % 2 * half, half), half), :size]
    low = jnp.concatenate([part.astype(jnp.bfloat16) for part in current], axis=1)
    phase = phase_ref[...].astype(jnp.bfloat16)
    weighted_t = jnp.dot(low, phase, preferred_element_type=jnp.float32)
    weighted = weighted_t.T
    work[:, :size] = contract(weighted_t, weighted_t, 1, 1)
    row_at = lax.broadcasted_iota(jnp.int32, (size, size), 0)
    col_at = lax.broadcasted_iota(jnp.int32, (size, size), 1)
    work[:, size:] = jnp.where(row_at == col_at, 1.0, 0.0)
    factor_and_invert(work, size)
    basis_ref[...] = contract(weighted, work[:, size:], 1, 1)


def local(right_side, factor_window, diag_inverse, phase_cov):
    row_count = lax.axis_size("row")
    col_count = lax.axis_size("col")
    row_index = lax.axis_index("row")
    col_index = lax.axis_index("col")
    block_rows = right_side.shape[0]
    rank_width = right_side.shape[1]
    col_width = factor_window.shape[1]
    chunk = rank_width // col_count
    vmem = pl.BlockSpec(memory_space=pltpu.VMEM)
    smem = pl.BlockSpec(memory_space=pltpu.SMEM)
    params = pltpu.CompilerParams(vmem_limit_bytes=VMEM_BYTES)
    col_scalar = col_index.astype(jnp.int32).reshape(1)
    piece = pl.pallas_call(
        prepare,
        out_shape=jax.ShapeDtypeStruct((col_width + chunk, block_rows), jnp.float32),
        in_specs=[smem, vmem, vmem, vmem],
        out_specs=vmem,
        scratch_shapes=[pltpu.VMEM((rank_width, block_rows), jnp.float32)],
        compiler_params=params,
    )(col_scalar, right_side, factor_window, diag_inverse)
    quarter = col_width // 2
    device = lambda row, col: row * col_count + col
    fold = [
        (device(row, 2 * j + core), device(row_count - 1 - row, 2 * (row_count - 1 - j) + core))
        for row in range(row_count)
        for j in range(row)
        for core in range(2)
    ]
    folded = lax.ppermute(piece[quarter:col_width], ("row", "col"), fold)
    kept = jnp.where(col_index // 2 < row_index, piece[:quarter], folded)
    message = jnp.concatenate([kept, piece[col_width:]], axis=0)
    chips = row_count * col_count // 2
    cores = [[2 * chip + core for chip in range(chips)] for core in range(2)]
    half_pieces = lax.all_to_all(
        jnp.broadcast_to(message[None], (chips,) + message.shape), ("row", "col"), 0, 0, axis_index_groups=cores, tiled=True
    )
    pairs = [[2 * j, 2 * j + 1] for j in range(col_count // 2)]
    pieces = lax.all_gather(half_pieces, "col", axis_index_groups=pairs)
    tile_count = phase_cov.shape[1] // TILE_ROWS
    cut = jnp.transpose(phase_cov.reshape(col_width, tile_count, TILE_ROWS), (1, 0, 2)).astype(jnp.float32)
    phase = lax.all_to_all(cut, "col", 0, 0, tiled=True).reshape(col_count * col_width, TILE_ROWS)
    basis, solved = pl.pallas_call(
        finish,
        out_shape=[
            jax.ShapeDtypeStruct((TILE_ROWS, rank_width), jnp.float32),
            jax.ShapeDtypeStruct((col_width, rank_width), jnp.float32),
        ],
        in_specs=[smem, vmem, vmem],
        out_specs=[vmem, vmem],
        scratch_shapes=[
            pltpu.VMEM((row_count, rank_width, block_rows), jnp.float32),
            pltpu.VMEM((rank_width, 2 * rank_width), jnp.float32),
        ],
        compiler_params=params,
    )(col_scalar, pieces, phase)
    basis = basis.reshape(col_count, TILE_ROWS // col_count, rank_width)
    return (lax.all_to_all(basis, "col", 0, 0, tiled=True), solved)


def solution(mesh):
    in_specs = (P("row", None), P("row", "col"), P("row", None), P("col", "row"))
    out_specs = (P("row", "col", None), P("col", None))
    return jax.shard_map(local, mesh=mesh, in_specs=in_specs, out_specs=out_specs, check_vma=False)
```

```python
import functools

import jax
import jax.numpy as jnp
from jax import lax
from jax.experimental import pallas as pl
from jax.experimental.pallas import tpu as pltpu
from jax.sharding import PartitionSpec as P

TILE_ROWS = 512
PANEL = 32
HIGHEST = lax.Precision.HIGHEST
VMEM_BYTES = 48 * 1024 * 1024


def contract(a, b, da, db):
    return lax.dot_general(a, b, (((da,), (db,)), ((), ())), precision=HIGHEST, preferred_element_type=jnp.float32)


def split(a):
    high = a.astype(jnp.bfloat16)
    return high, (a - high.astype(jnp.float32)).astype(jnp.bfloat16)


def dot3(a, b):
    dot = functools.partial(jnp.dot, preferred_element_type=jnp.float32)
    return dot(a[0], b[0]) + (dot(a[0], b[1]) + dot(a[1], b[0]))


def prepare(col_ref, right_ref, factor_ref, diag_ref, out_ref, scratch):
    diag = diag_ref[...]
    half = factor_ref.shape[1]
    chunk = out_ref.shape[0] - half
    out_ref[:half] = contract(factor_ref[...], diag, 0, 1)
    scratch[...] = contract(right_ref[...], diag, 0, 1)
    out_ref[half:] = scratch[pl.ds(pl.multiple_of(col_ref[0] * chunk, chunk), chunk), :]


def factor_and_invert(work, size):
    rows = lax.broadcasted_iota(jnp.int32, (PANEL, 1), 0)
    for start in range(0, size, PANEL):
        panel = work[start : start + PANEL, :]
        for k in range(PANEL):
            column = panel[:, start + k : start + k + 1]
            scale = lax.rsqrt(column[k : k + 1, :])
            row = panel[k : k + 1, :] * scale
            below = jnp.where(rows > k, column * scale, 0.0)
            panel = jnp.where(rows == k, row, panel - below * row)
        work[start : start + PANEL, :] = panel
        rest = start + PANEL
        if rest < size:
            work[rest:, :] -= contract(panel[:, rest:size], panel, 0, 0)


def block_solve(place_ref, own_ref, other_ref, low_ref, solved_ref, solved_t, work):
    turns, planes, rows, size = own_ref.shape
    blocks = turns * 2
    quarter = size // 4
    col, turn = place_ref[0], place_ref[1]
    core = col % 2

    def piece(block_row, block_col, half, start, stop):
        slot = (turn - block_row // 2 + turns) % turns
        at = block_row % 2 * blocks + block_col
        own, other = own_ref[slot, at, start:stop, :], other_ref[slot, at, start:stop, :]
        return jnp.where(core == half, own, other)

    current = []
    for i in range(blocks):
        parts = [piece(i, j, half, quarter, rows) for j in range(blocks) for half in range(2)]
        current.append(jnp.concatenate(parts, axis=0))
    for j in range(blocks):
        solved_t[j] = current[j]
        low_ref[:, j * size : (j + 1) * size] = current[j].astype(jnp.bfloat16)
        if j + 1 == blocks:
            break
        solved_pair = split(current[j])
        for i in range(j + 1, blocks):
            places = ((i, j), (blocks - 1 - i, blocks - 1 - j))
            parts = [piece(*at, half, 0, quarter) for half in range(2) for at in places]
            current[i] = current[i] - dot3(solved_pair, split(jnp.concatenate(parts, axis=0)))
    half_rows = solved_ref.shape[0]
    work[...] = solved_t[col // 2].T
    solved_ref[...] = work[pl.ds(pl.multiple_of(core * half_rows, half_rows), half_rows), :]


def tile_basis(low_ref, phase_ref, basis_ref, work):
    size = low_ref.shape[0]
    phase = phase_ref[...].astype(jnp.bfloat16)
    weighted_t = jnp.dot(low_ref[...], phase, preferred_element_type=jnp.float32)
    weighted = weighted_t.T
    work[:, :size] = contract(weighted_t, weighted_t, 1, 1)
    row_at = lax.broadcasted_iota(jnp.int32, (size, size), 0)
    col_at = lax.broadcasted_iota(jnp.int32, (size, size), 1)
    work[:, size:] = jnp.where(row_at == col_at, 1.0, 0.0)
    factor_and_invert(work, size)
    basis_ref[...] = contract(weighted, work[:, size:], 1, 1)


def local(right_side, factor_window, diag_inverse, phase_cov):
    row_count = lax.axis_size("row")
    col_count = lax.axis_size("col")
    row_index = lax.axis_index("row")
    col_index = lax.axis_index("col")
    block_rows = right_side.shape[0]
    rank_width = right_side.shape[1]
    col_width = factor_window.shape[1]
    chunk = rank_width // col_count
    turns = row_count // 2
    blocks = col_count // 2
    vmem = pl.BlockSpec(memory_space=pltpu.VMEM)
    smem = pl.BlockSpec(memory_space=pltpu.SMEM)
    params = pltpu.CompilerParams(vmem_limit_bytes=VMEM_BYTES)
    place = jnp.stack([col_index, row_index // 2]).astype(jnp.int32)
    piece = pl.pallas_call(
        prepare,
        out_shape=jax.ShapeDtypeStruct((col_width + chunk, block_rows), jnp.float32),
        in_specs=[smem, vmem, vmem, vmem],
        out_specs=vmem,
        scratch_shapes=[pltpu.VMEM((rank_width, block_rows), jnp.float32)],
        compiler_params=params,
    )(place, right_side, factor_window, diag_inverse)
    quarter = col_width // 2

    def device(row, col):
        return row * col_count + col

    fold = [
        (device(row, 2 * j + core), device(row_count - 1 - row, 2 * (blocks - 1 - j) + core))
        for row in range(row_count)
        for j in range(row)
        for core in range(2)
    ]
    folded = lax.ppermute(piece[quarter:col_width], ("row", "col"), fold)
    kept = jnp.where(col_index // 2 < row_index, piece[:quarter], folded)
    message = jnp.concatenate([kept, piece[col_width:]], axis=0)
    planes = [
        [device(2 * turn + low_bit, 2 * j + core) for low_bit in range(2) for j in range(blocks)]
        for turn in range(turns)
        for core in range(2)
    ]
    copies = jnp.broadcast_to(message[None], (2 * blocks,) + message.shape)
    plane = lax.all_to_all(copies, ("row", "col"), 0, 0, axis_index_groups=planes, tiled=True)
    tile_count = phase_cov.shape[1] // TILE_ROWS
    cut = jnp.transpose(phase_cov.reshape(col_width, tile_count, TILE_ROWS), (1, 0, 2)).astype(jnp.float32)
    plane, cut = lax.optimization_barrier((plane, cut))
    phase = lax.all_to_all(cut, "col", 0, 0, tiled=True).reshape(col_count * col_width, TILE_ROWS)
    slots = [plane]
    for step in range(1, turns):
        turn_on = [(2 * turn + bit, 2 * ((turn + step) % turns) + bit) for turn in range(turns) for bit in range(2)]
        slots.append(lax.ppermute(plane, "row", turn_on))
    own = jnp.stack(slots)
    other = lax.ppermute(own, "col", [(col, col ^ 1) for col in range(col_count)])
    low, solved = pl.pallas_call(
        block_solve,
        out_shape=[
            jax.ShapeDtypeStruct((rank_width, row_count * block_rows), jnp.bfloat16),
            jax.ShapeDtypeStruct((col_width, rank_width), jnp.float32),
        ],
        in_specs=[smem, vmem, vmem],
        out_specs=[vmem, vmem],
        scratch_shapes=[
            pltpu.VMEM((row_count, rank_width, block_rows), jnp.float32),
            pltpu.VMEM((rank_width, block_rows), jnp.float32),
        ],
        compiler_params=params,
        cost_estimate=pl.CostEstimate(flops=800_000_000, bytes_accessed=3_000_000, transcendentals=0),
    )(place, own, other)
    basis = pl.pallas_call(
        tile_basis,
        out_shape=jax.ShapeDtypeStruct((TILE_ROWS, rank_width), jnp.float32),
        in_specs=[vmem, vmem],
        out_specs=vmem,
        scratch_shapes=[pltpu.VMEM((rank_width, 2 * rank_width), jnp.float32)],
        compiler_params=params,
        cost_estimate=pl.CostEstimate(flops=1_000_000_000, bytes_accessed=3_000_000, transcendentals=0),
    )(low, phase)
    basis = basis.reshape(col_count, TILE_ROWS // col_count, rank_width)
    return (lax.all_to_all(basis, "col", 0, 0, tiled=True), solved)


def solution(mesh):
    in_specs = (P("row", None), P("row", "col"), P("row", None), P("col", "row"))
    out_specs = (P("row", "col", None), P("col", None))
    return jax.shard_map(local, mesh=mesh, in_specs=in_specs, out_specs=out_specs, check_vma=False)
```

```python
import functools

import jax
import jax.numpy as jnp
from jax import lax
from jax.experimental import pallas as pl
from jax.experimental.pallas import tpu as pltpu
from jax.sharding import PartitionSpec as P

TILE_ROWS = 512
PANEL = 32
HIGHEST = lax.Precision.HIGHEST
VMEM_BYTES = 48 * 1024 * 1024


def contract(a, b, da, db):
    return lax.dot_general(a, b, (((da,), (db,)), ((), ())), precision=HIGHEST, preferred_element_type=jnp.float32)


def split(a):
    high = a.astype(jnp.bfloat16)
    return high, (a - high.astype(jnp.float32)).astype(jnp.bfloat16)


def dot3(a, b):
    dot = functools.partial(jnp.dot, preferred_element_type=jnp.float32)
    return dot(a[0], b[0]) + (dot(a[0], b[1]) + dot(a[1], b[0]))


def prepare(col_ref, right_ref, factor_ref, diag_ref, out_ref, scratch):
    diag = diag_ref[...]
    half = factor_ref.shape[0]
    chunk = out_ref.shape[0] - half
    out_ref[:half] = contract(factor_ref[...], diag, 1, 1)
    scratch[...] = contract(right_ref[...], diag, 0, 1)
    out_ref[half:] = scratch[pl.ds(pl.multiple_of(col_ref[0] * chunk, chunk), chunk), :]


def factor_and_invert(work, size):
    rows = lax.broadcasted_iota(jnp.int32, (PANEL, 1), 0)
    for start in range(0, size, PANEL):
        panel = work[start : start + PANEL, :]
        for k in range(PANEL):
            column = panel[:, start + k : start + k + 1]
            scale = lax.rsqrt(column[k : k + 1, :])
            row = panel[k : k + 1, :] * scale
            below = jnp.where(rows > k, column * scale, 0.0)
            panel = jnp.where(rows == k, row, panel - below * row)
        work[start : start + PANEL, :] = panel
        rest = start + PANEL
        if rest < size:
            work[rest:, :] -= contract(panel[:, rest:size], panel, 0, 0)


def block_solve(place_ref, own_ref, other_ref, low_ref, solved_ref, solved_t, work):
    rows, size = own_ref.shape[1:]
    blocks = solved_t.shape[0]
    quarter = size // 4
    col, row = place_ref[0], place_ref[1]
    core = col % 2
    turn, ring, level = row // 2, col // 2 % 2 * 2 + row % 2, col // 4

    def piece(block_row, block_col, half, start, stop):
        steps = [(block_row // 2, turn), (block_col % 2 * 2 + block_row % 2, ring), (block_col // 2, level)]
        far = [jnp.bitwise_xor(here, there) for there, here in steps]
        at = far[0] * 16 + far[1] * 4 + far[2]
        own, other = own_ref[at, start:stop, :], other_ref[at, start:stop, :]
        return jnp.where(core == half, own, other)

    current = []
    for i in range(blocks):
        parts = [piece(i, j, half, quarter, rows) for j in range(blocks) for half in range(2)]
        current.append(jnp.concatenate(parts, axis=0))
    for j in range(blocks):
        solved_t[j] = current[j]
        low_ref[:, j * size : (j + 1) * size] = current[j].astype(jnp.bfloat16)
        if j + 1 == blocks:
            break
        solved_pair = split(current[j])
        for i in range(j + 1, blocks):
            places = ((i, j), (blocks - 1 - i, blocks - 1 - j))
            parts = [piece(*at, half, 0, quarter) for half in range(2) for at in places]
            current[i] = current[i] - dot3(solved_pair, split(jnp.concatenate(parts, axis=0)))
    half_rows = solved_ref.shape[0]
    work[...] = solved_t[col // 2].T
    solved_ref[...] = work[pl.ds(pl.multiple_of(core * half_rows, half_rows), half_rows), :]


def tile_basis(low_ref, phase_ref, basis_ref, work):
    size = low_ref.shape[0]
    phase = phase_ref[...].astype(jnp.bfloat16)
    weighted_t = jnp.dot(low_ref[...], phase, preferred_element_type=jnp.float32)
    weighted = weighted_t.T
    work[:, :size] = contract(weighted_t, weighted_t, 1, 1)
    row_at = lax.broadcasted_iota(jnp.int32, (size, size), 0)
    col_at = lax.broadcasted_iota(jnp.int32, (size, size), 1)
    work[:, size:] = jnp.where(row_at == col_at, 1.0, 0.0)
    factor_and_invert(work, size)
    basis_ref[...] = contract(weighted, work[:, size:], 1, 1)


def local(right_side, factor_window, diag_inverse, phase_cov):
    row_count = lax.axis_size("row")
    col_count = lax.axis_size("col")
    row_index = lax.axis_index("row")
    col_index = lax.axis_index("col")
    block_rows = right_side.shape[0]
    rank_width = right_side.shape[1]
    col_width = factor_window.shape[1]
    chunk = rank_width // col_count
    blocks = col_count // 2
    vmem = pl.BlockSpec(memory_space=pltpu.VMEM)
    smem = pl.BlockSpec(memory_space=pltpu.SMEM)
    params = pltpu.CompilerParams(vmem_limit_bytes=VMEM_BYTES)
    place = jnp.stack([col_index, row_index]).astype(jnp.int32)
    piece = pl.pallas_call(
        prepare,
        out_shape=jax.ShapeDtypeStruct((col_width + chunk, block_rows), jnp.float32),
        in_specs=[smem, vmem, vmem, vmem],
        out_specs=vmem,
        scratch_shapes=[pltpu.VMEM((rank_width, block_rows), jnp.float32)],
        compiler_params=params,
    )(place, right_side, factor_window.T, diag_inverse)
    quarter = col_width // 2

    def device(row, col):
        return row * col_count + col

    fold = [
        (device(row, 2 * j + core), device(row_count - 1 - row, 2 * (blocks - 1 - j) + core))
        for row in range(row_count)
        for j in range(row)
        for core in range(2)
    ]
    folded = lax.ppermute(piece[quarter:col_width], ("row", "col"), fold)
    kept = jnp.where(col_index // 2 < row_index, piece[:quarter], folded)
    message = jnp.concatenate([kept, piece[col_width:]], axis=0)
    tile_count = phase_cov.shape[1] // TILE_ROWS
    cut = jnp.transpose(phase_cov.reshape(col_width, tile_count, TILE_ROWS), (1, 0, 2)).astype(jnp.float32)
    phase = lax.all_to_all(cut, "col", 0, 0, tiled=True).reshape(col_count * col_width, TILE_ROWS)
    by_level = [[(device(row, col), device(row, col ^ 4 * mask)) for row in range(row_count) for col in range(col_count)] for mask in range(1, 4)]
    by_ring = [
        [(device(row, col), device(row ^ mask % 2, col ^ mask // 2 * 2)) for row in range(row_count) for col in range(col_count)]
        for mask in range(1, 4)
    ]
    by_turn = [[(device(row, col), device(row ^ 2 * mask, col)) for row in range(row_count) for col in range(col_count)] for mask in range(1, 4)]
    own = message[None]
    for routes in (by_level, by_ring, by_turn):
        own = jnp.concatenate([own] + [lax.ppermute(own, ("row", "col"), route) for route in routes], axis=0)
    other = lax.ppermute(own, "col", [(col, col ^ 1) for col in range(col_count)])
    low, solved = pl.pallas_call(
        block_solve,
        out_shape=[
            jax.ShapeDtypeStruct((rank_width, row_count * block_rows), jnp.bfloat16),
            jax.ShapeDtypeStruct((col_width, rank_width), jnp.float32),
        ],
        in_specs=[smem, vmem, vmem],
        out_specs=[vmem, vmem],
        scratch_shapes=[
            pltpu.VMEM((row_count, rank_width, block_rows), jnp.float32),
            pltpu.VMEM((rank_width, block_rows), jnp.float32),
        ],
        compiler_params=params,
        cost_estimate=pl.CostEstimate(flops=800_000_000, bytes_accessed=3_000_000, transcendentals=0),
    )(place, own, other)
    basis = pl.pallas_call(
        tile_basis,
        out_shape=jax.ShapeDtypeStruct((TILE_ROWS, rank_width), jnp.float32),
        in_specs=[vmem, vmem],
        out_specs=vmem,
        scratch_shapes=[pltpu.VMEM((rank_width, 2 * rank_width), jnp.float32)],
        compiler_params=params,
        cost_estimate=pl.CostEstimate(flops=1_000_000_000, bytes_accessed=3_000_000, transcendentals=0),
    )(low, phase)
    basis = basis.reshape(col_count, TILE_ROWS // col_count, rank_width)
    return (lax.all_to_all(basis, "col", 0, 0, tiled=True), solved)


def solution(mesh):
    in_specs = (P("row", None), P("row", "col"), P("row", None), P("col", "row"))
    out_specs = (P("row", "col", None), P("col", None))
    return jax.shard_map(local, mesh=mesh, in_specs=in_specs, out_specs=out_specs, check_vma=False)
```

```python
import functools

import jax
import jax.numpy as jnp
from jax import lax
from jax.experimental import pallas as pl
from jax.experimental.pallas import tpu as pltpu
from jax.sharding import PartitionSpec as P

TILE_ROWS = 512
PANEL = 32
SUBLANES = 8
HIGHEST = lax.Precision.HIGHEST
VMEM_BYTES = 48 * 1024 * 1024


def contract(a, b, da, db):
    return lax.dot_general(a, b, (((da,), (db,)), ((), ())), precision=HIGHEST, preferred_element_type=jnp.float32)


def split(a):
    high = a.astype(jnp.bfloat16)
    return high, (a - high.astype(jnp.float32)).astype(jnp.bfloat16)


def dot3(a, b):
    dot = functools.partial(jnp.dot, preferred_element_type=jnp.float32)
    return dot(a[0], b[0]) + (dot(a[0], b[1]) + dot(a[1], b[0]))


def prepare(place_ref, right_hbm, factor_hbm, diag_hbm, out_ref, right, factor, diag, scratch, arrived):
    sources = ((diag_hbm, diag), (factor_hbm, factor), (right_hbm, right))
    copies = [pltpu.make_async_copy(source, target, arrived.at[i]) for i, (source, target) in enumerate(sources)]
    for copy in copies:
        copy.start()
    for copy in copies:
        copy.wait()
    half = factor.shape[0]
    chunk = out_ref.shape[0] - half
    out_ref[:half] = contract(factor[...], diag[...], 1, 1)
    scratch[...] = contract(right[...], diag[...], 0, 1)
    out_ref[half:] = scratch[pl.ds(pl.multiple_of(place_ref[0] * chunk, chunk), chunk), :]


def factor_and_invert(work, size):
    shape = (SUBLANES, size)
    lane = lax.broadcasted_iota(jnp.int32, shape, 1)
    sublane = lax.broadcasted_iota(jnp.int32, shape, 0)
    for start in range(0, size, PANEL):
        end = start + PANEL
        groups = [work[at : at + SUBLANES, :] for at in range(start, end, SUBLANES)]
        for g in range(len(groups)):
            first = start + g * SUBLANES
            inside = (lane >= first) & (lane < first + SUBLANES)
            columns = [jnp.broadcast_to(groups[g][:, first + j : first + j + 1], shape) for j in range(SUBLANES)]
            pivot = {(i, j): jnp.broadcast_to(columns[j][i : i + 1, :], shape) for j in range(SUBLANES) for i in range(j, SUBLANES)}
            rows, scales = [], []
            for i in range(SUBLANES):
                row = jnp.broadcast_to(groups[g][i : i + 1, :], shape)
                rows.append(jnp.where(inside, jnp.where(lane == first + i, 1.0, 0.0), row))
            for j in range(SUBLANES):
                scale = lax.rsqrt(pivot[j, j])
                scales.append(scale)
                rows[j] = rows[j] * scale
                for i in range(j + 1, SUBLANES):
                    pivot[i, j] = pivot[i, j] * scale
                for i in range(j + 1, SUBLANES):
                    for k in range(j + 1, i + 1):
                        pivot[i, k] = pivot[i, k] - pivot[i, j] * pivot[k, j]
                    rows[i] = rows[i] - pivot[i, j] * rows[j]
            merged = rows[0]
            for i in range(1, SUBLANES):
                merged = jnp.where(sublane == i, rows[i], merged)
            groups[g] = merged
            for h in range(g + 1, len(groups)):
                left = []
                rest = jnp.where(inside, 0.0, groups[h])
                for j in range(SUBLANES):
                    column = jnp.broadcast_to(groups[h][:, first + j : first + j + 1], shape)
                    for i in range(j):
                        column = column - left[i] * pivot[j, i]
                    left.append(column * scales[j])
                    rest = rest - left[j] * rows[j]
                groups[h] = rest
        panel = jnp.concatenate(groups, axis=0)
        work[start:end, :] = panel
        if end < size:
            row_lane = lax.broadcasted_iota(jnp.int32, (size - end, size), 1)
            rest = jnp.where((row_lane >= start) & (row_lane < end), 0.0, work[end:, :])
            panel_lane = lax.broadcasted_iota(jnp.int32, panel.shape, 1)
            panel_row = lax.broadcasted_iota(jnp.int32, panel.shape, 0) + start
            known = jnp.where((panel_lane <= panel_row) | (panel_lane >= end), panel, 0.0)
            work[end:, :] = rest - contract(panel, known, 0, 0)[end:, :]
    square = (size, size)
    lower = lax.broadcasted_iota(jnp.int32, square, 1) <= lax.broadcasted_iota(jnp.int32, square, 0)
    work[...] = jnp.where(lower, work[...], 0.0)


def block_solve(place_ref, own_ref, other_ref, low_ref, solved_ref, solved_t, work):
    turns, planes, rows, size = own_ref.shape
    blocks = turns * 2
    quarter = size // 4
    col, turn = place_ref[0], place_ref[1]
    core = col % 2

    def piece(block_row, block_col, half, start, stop):
        slot = (turn - block_row // 2 + turns) % turns
        at = block_row % 2 * blocks + block_col
        own, other = own_ref[slot, at, start:stop, :], other_ref[slot, at, start:stop, :]
        return jnp.where(core == half, own, other)

    current = []
    for i in range(blocks):
        parts = [piece(i, j, half, quarter, rows) for j in range(blocks) for half in range(2)]
        current.append(jnp.concatenate(parts, axis=0))
    for j in range(blocks):
        solved_t[j] = current[j]
        low_ref[:, j * size : (j + 1) * size] = current[j].astype(jnp.bfloat16)
        if j + 1 == blocks:
            break
        solved_pair = split(current[j])
        for i in range(j + 1, blocks):
            places = ((i, j), (blocks - 1 - i, blocks - 1 - j))
            parts = [piece(*at, half, 0, quarter) for half in range(2) for at in places]
            current[i] = current[i] - dot3(solved_pair, split(jnp.concatenate(parts, axis=0)))
    half_rows = solved_ref.shape[0]
    work[...] = solved_t[col // 2].T
    solved_ref[...] = work[pl.ds(pl.multiple_of(core * half_rows, half_rows), half_rows), :]


def tile_basis(low_ref, phase_ref, basis_ref, work):
    size = low_ref.shape[0]
    phase = phase_ref[...].astype(jnp.bfloat16)
    weighted_t = jnp.dot(low_ref[...], phase, preferred_element_type=jnp.float32)
    weighted = weighted_t.T
    work[...] = contract(weighted_t, weighted_t, 1, 1)
    factor_and_invert(work, size)
    basis_ref[...] = contract(weighted, work[...], 1, 1)


def local(right_side, factor_window, diag_inverse, phase_cov):
    row_count = lax.axis_size("row")
    col_count = lax.axis_size("col")
    row_index = lax.axis_index("row")
    col_index = lax.axis_index("col")
    block_rows = right_side.shape[0]
    rank_width = right_side.shape[1]
    col_width = factor_window.shape[1]
    chunk = rank_width // col_count
    turns = row_count // 2
    blocks = col_count // 2
    vmem = pl.BlockSpec(memory_space=pltpu.VMEM)
    smem = pl.BlockSpec(memory_space=pltpu.SMEM)
    params = pltpu.CompilerParams(vmem_limit_bytes=VMEM_BYTES)
    place = jnp.stack([col_index, row_index // 2]).astype(jnp.int32)
    piece = pl.pallas_call(
        prepare,
        out_shape=jax.ShapeDtypeStruct((col_width + chunk, block_rows), jnp.float32),
        in_specs=[smem] + [pl.BlockSpec(memory_space=pltpu.HBM)] * 3,
        out_specs=vmem,
        scratch_shapes=[
            pltpu.VMEM(right_side.shape, jnp.float32),
            pltpu.VMEM((col_width, block_rows), jnp.float32),
            pltpu.VMEM(diag_inverse.shape, jnp.float32),
            pltpu.VMEM((rank_width, block_rows), jnp.float32),
            pltpu.SemaphoreType.DMA((3,)),
        ],
        compiler_params=pltpu.CompilerParams(vmem_limit_bytes=64 * 1024 * 1024 - 128 * 1024),
    )(place, right_side, factor_window.T, diag_inverse)
    quarter = col_width // 2

    def device(row, col):
        return row * col_count + col

    fold = [
        (device(row, 2 * j + core), device(row_count - 1 - row, 2 * (blocks - 1 - j) + core))
        for row in range(row_count)
        for j in range(row)
        for core in range(2)
    ]
    folded = lax.ppermute(piece[quarter:col_width], ("row", "col"), fold)
    kept = jnp.where(col_index // 2 < row_index, piece[:quarter], folded)
    message = jnp.concatenate([kept, piece[col_width:]], axis=0)
    planes = [
        [device(2 * turn + low_bit, 2 * j + core) for low_bit in range(2) for j in range(blocks)]
        for turn in range(turns)
        for core in range(2)
    ]
    copies = jnp.broadcast_to(message[None], (2 * blocks,) + message.shape)
    plane = lax.all_to_all(copies, ("row", "col"), 0, 0, axis_index_groups=planes, tiled=True)
    tile_count = phase_cov.shape[1] // TILE_ROWS
    cut = jnp.transpose(phase_cov.reshape(col_width, tile_count, TILE_ROWS), (1, 0, 2)).astype(jnp.float32)
    plane, cut = lax.optimization_barrier((plane, cut))
    phase = lax.all_to_all(cut, "col", 0, 0, tiled=True).reshape(col_count * col_width, TILE_ROWS)
    slots = [plane]
    for step in range(1, turns):
        turn_on = [(2 * turn + bit, 2 * ((turn + step) % turns) + bit) for turn in range(turns) for bit in range(2)]
        slots.append(lax.ppermute(plane, "row", turn_on))
    own = jnp.stack(slots)
    other = lax.ppermute(own, "col", [(col, col ^ 1) for col in range(col_count)])
    low, solved = pl.pallas_call(
        block_solve,
        out_shape=[
            jax.ShapeDtypeStruct((rank_width, row_count * block_rows), jnp.bfloat16),
            jax.ShapeDtypeStruct((col_width, rank_width), jnp.float32),
        ],
        in_specs=[smem, vmem, vmem],
        out_specs=[vmem, vmem],
        scratch_shapes=[
            pltpu.VMEM((row_count, rank_width, block_rows), jnp.float32),
            pltpu.VMEM((rank_width, block_rows), jnp.float32),
        ],
        compiler_params=params,
        cost_estimate=pl.CostEstimate(flops=800_000_000, bytes_accessed=3_000_000, transcendentals=0),
    )(place, own, other)
    basis = pl.pallas_call(
        tile_basis,
        out_shape=jax.ShapeDtypeStruct((TILE_ROWS, rank_width), jnp.float32),
        in_specs=[vmem, vmem],
        out_specs=vmem,
        scratch_shapes=[pltpu.VMEM((rank_width, rank_width), jnp.float32)],
        compiler_params=params,
        cost_estimate=pl.CostEstimate(flops=1_000_000_000, bytes_accessed=3_000_000, transcendentals=0),
    )(low, phase)
    basis = basis.reshape(col_count, TILE_ROWS // col_count, rank_width)
    return (lax.all_to_all(basis, "col", 0, 0, tiled=True), solved)


def solution(mesh):
    in_specs = (P("row", None), P("row", "col"), P("row", None), P("col", "row"))
    out_specs = (P("row", "col", None), P("col", None))
    return jax.shard_map(local, mesh=mesh, in_specs=in_specs, out_specs=out_specs, check_vma=False)
```

```python
import functools

import jax
import jax.numpy as jnp
from jax import lax
from jax.experimental import pallas as pl
from jax.experimental.pallas import tpu as pltpu
from jax.sharding import PartitionSpec as P

TILE_ROWS = 512
PANEL = 32
SUBLANES = 8
HIGHEST = lax.Precision.HIGHEST
VMEM_BYTES = 48 * 1024 * 1024


def contract(a, b, da, db):
    return lax.dot_general(a, b, (((da,), (db,)), ((), ())), precision=HIGHEST, preferred_element_type=jnp.float32)


def split(a):
    high = a.astype(jnp.bfloat16)
    return high, (a - high.astype(jnp.float32)).astype(jnp.bfloat16)


def dot3(a, b):
    dot = functools.partial(jnp.dot, preferred_element_type=jnp.float32)
    return dot(a[0], b[0]) + (dot(a[0], b[1]) + dot(a[1], b[0]))


def prepare(right_hbm, factor_hbm, diag_hbm, message_ref, send_ref, right, factor, diag, scratch, arrived):
    sources = ((diag_hbm, diag), (factor_hbm, factor), (right_hbm, right))
    copies = [pltpu.make_async_copy(source, target, arrived.at[i]) for i, (source, target) in enumerate(sources)]
    for copy in copies:
        copy.start()
    for copy in copies:
        copy.wait()
    quarter = send_ref.shape[0]
    chunk = message_ref.shape[0] - quarter
    scaled = contract(factor[...], diag[...], 1, 1)
    message_ref[:quarter] = scaled[:quarter]
    send_ref[...] = scaled[quarter:]
    scratch[...] = contract(right[...], diag[...], 0, 1)
    message_ref[quarter:] = scratch[pl.ds(pl.multiple_of(lax.axis_index("col") * chunk, chunk), chunk), :]


def spread(message_ref, folded_ref, out_ref):
    quarter = folded_ref.shape[0]
    keeps = lax.axis_index("col") // 2 < lax.axis_index("row")
    top = jnp.where(keeps, message_ref[:quarter], folded_ref[...])
    bottom = message_ref[quarter:]
    for at in range(out_ref.shape[0]):
        out_ref[at, :quarter] = top
        out_ref[at, quarter:] = bottom


def factor_and_invert(work, size):
    shape = (SUBLANES, size)
    lane = lax.broadcasted_iota(jnp.int32, shape, 1)
    sublane = lax.broadcasted_iota(jnp.int32, shape, 0)
    for start in range(0, size, PANEL):
        end = start + PANEL
        groups = [work[at : at + SUBLANES, :] for at in range(start, end, SUBLANES)]
        for g in range(len(groups)):
            first = start + g * SUBLANES
            inside = (lane >= first) & (lane < first + SUBLANES)
            columns = [jnp.broadcast_to(groups[g][:, first + j : first + j + 1], shape) for j in range(SUBLANES)]
            pivot = {(i, j): jnp.broadcast_to(columns[j][i : i + 1, :], shape) for j in range(SUBLANES) for i in range(j, SUBLANES)}
            rows, scales = [], []
            for i in range(SUBLANES):
                row = jnp.broadcast_to(groups[g][i : i + 1, :], shape)
                rows.append(jnp.where(inside, jnp.where(lane == first + i, 1.0, 0.0), row))
            for j in range(SUBLANES):
                scale = lax.rsqrt(pivot[j, j])
                scales.append(scale)
                rows[j] = rows[j] * scale
                for i in range(j + 1, SUBLANES):
                    pivot[i, j] = pivot[i, j] * scale
                for i in range(j + 1, SUBLANES):
                    for k in range(j + 1, i + 1):
                        pivot[i, k] = pivot[i, k] - pivot[i, j] * pivot[k, j]
                    rows[i] = rows[i] - pivot[i, j] * rows[j]
            merged = rows[0]
            for i in range(1, SUBLANES):
                merged = jnp.where(sublane == i, rows[i], merged)
            groups[g] = merged
            for h in range(g + 1, len(groups)):
                left = []
                rest = jnp.where(inside, 0.0, groups[h])
                for j in range(SUBLANES):
                    column = jnp.broadcast_to(groups[h][:, first + j : first + j + 1], shape)
                    for i in range(j):
                        column = column - left[i] * pivot[j, i]
                    left.append(column * scales[j])
                    rest = rest - left[j] * rows[j]
                groups[h] = rest
        panel = jnp.concatenate(groups, axis=0)
        work[start:end, :] = panel
        if end < size:
            row_lane = lax.broadcasted_iota(jnp.int32, (size - end, size), 1)
            rest = jnp.where((row_lane >= start) & (row_lane < end), 0.0, work[end:, :])
            panel_lane = lax.broadcasted_iota(jnp.int32, panel.shape, 1)
            panel_row = lax.broadcasted_iota(jnp.int32, panel.shape, 0) + start
            known = jnp.where((panel_lane <= panel_row) | (panel_lane >= end), panel, 0.0)
            work[end:, :] = rest - contract(panel, known, 0, 0)[end:, :]
    square = (size, size)
    lower = lax.broadcasted_iota(jnp.int32, square, 1) <= lax.broadcasted_iota(jnp.int32, square, 0)
    work[...] = jnp.where(lower, work[...], 0.0)


def block_solve(own_ref, other_ref, low_ref, solved_ref, solved_t, work):
    turns, planes, rows, size = own_ref.shape
    blocks = turns * 2
    quarter = size // 4
    col, row = lax.axis_index("col"), lax.axis_index("row")
    turn, low_bit = row // 2, row % 2
    core = col % 2

    def piece(block_row, block_col, half, start, stop):
        slot = (turn - block_row // 2 + turns) % turns
        at = jnp.bitwise_xor(block_row % 2, low_bit) * blocks + block_col
        own, other = own_ref[slot, at, start:stop, :], other_ref[slot, at, start:stop, :]
        return jnp.where(core == half, own, other)

    current = []
    for i in range(blocks):
        parts = [piece(i, j, half, quarter, rows) for j in range(blocks) for half in range(2)]
        current.append(jnp.concatenate(parts, axis=0))
    for j in range(blocks):
        solved_t[j] = current[j]
        low_ref[:, j * size : (j + 1) * size] = current[j].astype(jnp.bfloat16)
        if j + 1 == blocks:
            break
        solved_pair = split(current[j])
        for i in range(j + 1, blocks):
            places = ((i, j), (blocks - 1 - i, blocks - 1 - j))
            parts = [piece(*at, half, 0, quarter) for half in range(2) for at in places]
            current[i] = current[i] - dot3(solved_pair, split(jnp.concatenate(parts, axis=0)))
    half_rows = solved_ref.shape[0]
    work[...] = solved_t[col // 2].T
    solved_ref[...] = work[pl.ds(pl.multiple_of(core * half_rows, half_rows), half_rows), :]


def tile_basis(low_ref, phase_ref, basis_ref, work):
    size = low_ref.shape[0]
    phase = phase_ref[...].astype(jnp.bfloat16)
    weighted_t = jnp.dot(low_ref[...], phase, preferred_element_type=jnp.float32)
    weighted = weighted_t.T
    work[...] = contract(weighted_t, weighted_t, 1, 1)
    factor_and_invert(work, size)
    basis_ref[...] = contract(weighted, work[...], 1, 1)


def local(right_side, factor_window, diag_inverse, phase_cov):
    row_count = lax.axis_size("row")
    col_count = lax.axis_size("col")
    block_rows = right_side.shape[0]
    rank_width = right_side.shape[1]
    col_width = factor_window.shape[1]
    chunk = rank_width // col_count
    turns = row_count // 2
    blocks = col_count // 2
    vmem = pl.BlockSpec(memory_space=pltpu.VMEM)
    params = pltpu.CompilerParams(vmem_limit_bytes=VMEM_BYTES)
    quarter = col_width // 2
    message, send = pl.pallas_call(
        prepare,
        out_shape=[
            jax.ShapeDtypeStruct((quarter + chunk, block_rows), jnp.float32),
            jax.ShapeDtypeStruct((quarter, block_rows), jnp.float32),
        ],
        in_specs=[pl.BlockSpec(memory_space=pltpu.HBM)] * 3,
        out_specs=[vmem, vmem],
        scratch_shapes=[
            pltpu.VMEM(right_side.shape, jnp.float32),
            pltpu.VMEM((col_width, block_rows), jnp.float32),
            pltpu.VMEM(diag_inverse.shape, jnp.float32),
            pltpu.VMEM((rank_width, block_rows), jnp.float32),
            pltpu.SemaphoreType.DMA((3,)),
        ],
        compiler_params=pltpu.CompilerParams(vmem_limit_bytes=64 * 1024 * 1024 - 128 * 1024),
    )(right_side, factor_window.T, diag_inverse)

    def device(row, col):
        return row * col_count + col

    fold = [
        (device(row, 2 * j + core), device(row_count - 1 - row, 2 * (blocks - 1 - j) + core))
        for row in range(row_count)
        for j in range(row)
        for core in range(2)
    ]
    folded = lax.ppermute(send, ("row", "col"), fold)
    copies = pl.pallas_call(
        spread,
        out_shape=jax.ShapeDtypeStruct((blocks,) + message.shape, jnp.float32),
        in_specs=[vmem, vmem],
        out_specs=vmem,
        compiler_params=params,
    )(message, folded)
    levels = [[2 * j + core for j in range(blocks)] for core in range(2)]
    plane = lax.all_to_all(copies, "col", 0, 0, axis_index_groups=levels, tiled=True)
    tile_count = phase_cov.shape[1] // TILE_ROWS
    cut = jnp.transpose(phase_cov.reshape(col_width, tile_count, TILE_ROWS), (1, 0, 2)).astype(jnp.float32)
    plane, cut = lax.optimization_barrier((plane, cut))
    phase = lax.all_to_all(cut, "col", 0, 0, tiled=True).reshape(col_count * col_width, TILE_ROWS)
    beside = lax.ppermute(plane, "row", [(row, row ^ 1) for row in range(row_count)])
    plane = jnp.concatenate([plane, beside], axis=0)
    slots = [plane]
    for step in range(1, turns):
        turn_on = [(2 * turn + bit, 2 * ((turn + step) % turns) + bit) for turn in range(turns) for bit in range(2)]
        slots.append(lax.ppermute(plane, "row", turn_on))
    own = jnp.stack(slots)
    other = lax.ppermute(own, "col", [(col, col ^ 1) for col in range(col_count)])
    low, solved = pl.pallas_call(
        block_solve,
        out_shape=[
            jax.ShapeDtypeStruct((rank_width, row_count * block_rows), jnp.bfloat16),
            jax.ShapeDtypeStruct((col_width, rank_width), jnp.float32),
        ],
        in_specs=[vmem, vmem],
        out_specs=[vmem, vmem],
        scratch_shapes=[
            pltpu.VMEM((row_count, rank_width, block_rows), jnp.float32),
            pltpu.VMEM((rank_width, block_rows), jnp.float32),
        ],
        compiler_params=params,
        cost_estimate=pl.CostEstimate(flops=800_000_000, bytes_accessed=3_000_000, transcendentals=0),
    )(own, other)
    basis = pl.pallas_call(
        tile_basis,
        out_shape=jax.ShapeDtypeStruct((TILE_ROWS, rank_width), jnp.float32),
        in_specs=[vmem, vmem],
        out_specs=vmem,
        scratch_shapes=[pltpu.VMEM((rank_width, rank_width), jnp.float32)],
        compiler_params=params,
        cost_estimate=pl.CostEstimate(flops=1_000_000_000, bytes_accessed=3_000_000, transcendentals=0),
    )(low, phase)
    basis = basis.reshape(col_count, TILE_ROWS // col_count, rank_width)
    return (lax.all_to_all(basis, "col", 0, 0, tiled=True), solved)


def solution(mesh):
    in_specs = (P("row", None), P("row", "col"), P("row", None), P("col", "row"))
    out_specs = (P("row", "col", None), P("col", None))
    return jax.shard_map(local, mesh=mesh, in_specs=in_specs, out_specs=out_specs, check_vma=False)
```

```python
import functools

import jax
import jax.numpy as jnp
from jax import lax
from jax.experimental import pallas as pl
from jax.experimental.pallas import tpu as pltpu
from jax.sharding import PartitionSpec as P

TILE_ROWS = 512
PANEL = 32
SUBLANES = 8
HIGHEST = lax.Precision.HIGHEST
VMEM_BYTES = 48 * 1024 * 1024


def contract(a, b, da, db):
    return lax.dot_general(a, b, (((da,), (db,)), ((), ())), precision=HIGHEST, preferred_element_type=jnp.float32)


def split(a):
    high = a.astype(jnp.bfloat16)
    return high, (a - high.astype(jnp.float32)).astype(jnp.bfloat16)


def dot3(a, b):
    dot = functools.partial(jnp.dot, preferred_element_type=jnp.float32)
    return dot(a[0], b[0]) + (dot(a[0], b[1]) + dot(a[1], b[0]))


def partner(row, col):
    bits = 1 if row // 2 == col // 2 else 6
    return row ^ bits, col ^ bits


def prepare(right_hbm, factor_hbm, diag_hbm, message_ref, send_ref, right, factor, diag, scratch, arrived):
    sources = ((diag_hbm, diag), (factor_hbm, factor), (right_hbm, right))
    copies = [pltpu.make_async_copy(source, target, arrived.at[i]) for i, (source, target) in enumerate(sources)]
    for copy in copies:
        copy.start()
    for copy in copies:
        copy.wait()
    quarter = send_ref.shape[0]
    chunk = message_ref.shape[0] - quarter
    scaled = contract(factor[...], diag[...], 1, 1)
    message_ref[:quarter] = scaled[:quarter]
    send_ref[...] = scaled[quarter:]
    scratch[...] = contract(right[...], diag[...], 0, 1)
    message_ref[quarter:] = scratch[pl.ds(pl.multiple_of(lax.axis_index("col") * chunk, chunk), chunk), :]


def spread(message_ref, folded_ref, out_ref):
    quarter = folded_ref.shape[0]
    keeps = lax.axis_index("col") // 2 < lax.axis_index("row")
    top = jnp.where(keeps, message_ref[:quarter], folded_ref[...])
    bottom = message_ref[quarter:]
    for at in range(out_ref.shape[0]):
        out_ref[at, :quarter] = top
        out_ref[at, quarter:] = bottom


def factor_and_invert(work, size):
    shape = (SUBLANES, size)
    lane = lax.broadcasted_iota(jnp.int32, shape, 1)
    sublane = lax.broadcasted_iota(jnp.int32, shape, 0)
    for start in range(0, size, PANEL):
        end = start + PANEL
        groups = [work[at : at + SUBLANES, :] for at in range(start, end, SUBLANES)]
        for g in range(len(groups)):
            first = start + g * SUBLANES
            inside = (lane >= first) & (lane < first + SUBLANES)
            columns = [jnp.broadcast_to(groups[g][:, first + j : first + j + 1], shape) for j in range(SUBLANES)]
            pivot = {(i, j): jnp.broadcast_to(columns[j][i : i + 1, :], shape) for j in range(SUBLANES) for i in range(j, SUBLANES)}
            rows, scales = [], []
            for i in range(SUBLANES):
                row = jnp.broadcast_to(groups[g][i : i + 1, :], shape)
                rows.append(jnp.where(inside, jnp.where(lane == first + i, 1.0, 0.0), row))
            for j in range(SUBLANES):
                scale = lax.rsqrt(pivot[j, j])
                scales.append(scale)
                rows[j] = rows[j] * scale
                for i in range(j + 1, SUBLANES):
                    pivot[i, j] = pivot[i, j] * scale
                for i in range(j + 1, SUBLANES):
                    for k in range(j + 1, i + 1):
                        pivot[i, k] = pivot[i, k] - pivot[i, j] * pivot[k, j]
                    rows[i] = rows[i] - pivot[i, j] * rows[j]
            merged = rows[0]
            for i in range(1, SUBLANES):
                merged = jnp.where(sublane == i, rows[i], merged)
            groups[g] = merged
            for h in range(g + 1, len(groups)):
                left = []
                rest = jnp.where(inside, 0.0, groups[h])
                for j in range(SUBLANES):
                    column = jnp.broadcast_to(groups[h][:, first + j : first + j + 1], shape)
                    for i in range(j):
                        column = column - left[i] * pivot[j, i]
                    left.append(column * scales[j])
                    rest = rest - left[j] * rows[j]
                groups[h] = rest
        panel = jnp.concatenate(groups, axis=0)
        work[start:end, :] = panel
        if end < size:
            row_lane = lax.broadcasted_iota(jnp.int32, (size - end, size), 1)
            rest = jnp.where((row_lane >= start) & (row_lane < end), 0.0, work[end:, :])
            panel_lane = lax.broadcasted_iota(jnp.int32, panel.shape, 1)
            panel_row = lax.broadcasted_iota(jnp.int32, panel.shape, 0) + start
            known = jnp.where((panel_lane <= panel_row) | (panel_lane >= end), panel, 0.0)
            work[end:, :] = rest - contract(panel, known, 0, 0)[end:, :]
    square = (size, size)
    lower = lax.broadcasted_iota(jnp.int32, square, 1) <= lax.broadcasted_iota(jnp.int32, square, 0)
    work[...] = jnp.where(lower, work[...], 0.0)


def block_solve(own_ref, other_ref, low_ref, solved_ref, solved_t, work):
    turns, planes, rows, size = own_ref.shape
    blocks = turns * 2
    quarter = size // 4
    col, row = lax.axis_index("col"), lax.axis_index("row")
    turn = row // 2
    core = col % 2

    def piece(block_row, block_col, half, start, stop):
        slot = (turn - block_row // 2 + turns) % turns
        at = block_row % 2 * blocks + block_col
        own, other = own_ref[slot, at, start:stop, :], other_ref[slot, at, start:stop, :]
        return jnp.where(core == half, own, other)

    current = []
    for i in range(blocks):
        parts = [piece(i, j, half, quarter, rows) for j in range(blocks) for half in range(2)]
        current.append(jnp.concatenate(parts, axis=0))
    for j in range(blocks):
        solved_t[j] = current[j]
        low_ref[:, j * size : (j + 1) * size] = current[j].astype(jnp.bfloat16)
        if j + 1 == blocks:
            break
        solved_pair = split(current[j])
        for i in range(j + 1, blocks):
            places = ((i, j), partner(i, j))
            parts = [piece(*at, half, 0, quarter) for half in range(2) for at in places]
            current[i] = current[i] - dot3(solved_pair, split(jnp.concatenate(parts, axis=0)))
    half_rows = solved_ref.shape[0]
    work[...] = solved_t[col // 2].T
    solved_ref[...] = work[pl.ds(pl.multiple_of(core * half_rows, half_rows), half_rows), :]


def tile_basis(low_ref, phase_ref, basis_ref, work):
    size = low_ref.shape[0]
    phase = phase_ref[...].astype(jnp.bfloat16)
    weighted_t = jnp.dot(low_ref[...], phase, preferred_element_type=jnp.float32)
    weighted = weighted_t.T
    work[...] = contract(weighted_t, weighted_t, 1, 1)
    factor_and_invert(work, size)
    basis_ref[...] = contract(weighted, work[...], 1, 1)


def local(right_side, factor_window, diag_inverse, phase_cov):
    row_count = lax.axis_size("row")
    col_count = lax.axis_size("col")
    block_rows = right_side.shape[0]
    rank_width = right_side.shape[1]
    col_width = factor_window.shape[1]
    chunk = rank_width // col_count
    turns = row_count // 2
    blocks = col_count // 2
    vmem = pl.BlockSpec(memory_space=pltpu.VMEM)
    params = pltpu.CompilerParams(vmem_limit_bytes=VMEM_BYTES)
    quarter = col_width // 2
    message, send = pl.pallas_call(
        prepare,
        out_shape=[
            jax.ShapeDtypeStruct((quarter + chunk, block_rows), jnp.float32),
            jax.ShapeDtypeStruct((quarter, block_rows), jnp.float32),
        ],
        in_specs=[pl.BlockSpec(memory_space=pltpu.HBM)] * 3,
        out_specs=[vmem, vmem],
        scratch_shapes=[
            pltpu.VMEM(right_side.shape, jnp.float32),
            pltpu.VMEM((col_width, block_rows), jnp.float32),
            pltpu.VMEM(diag_inverse.shape, jnp.float32),
            pltpu.VMEM((rank_width, block_rows), jnp.float32),
            pltpu.SemaphoreType.DMA((3,)),
        ],
        compiler_params=pltpu.CompilerParams(vmem_limit_bytes=64 * 1024 * 1024 - 128 * 1024),
    )(right_side, factor_window.T, diag_inverse)

    def device(row, col):
        return row * col_count + col

    fold = [
        (device(row, 2 * j + core), device(partner(row, j)[0], 2 * partner(row, j)[1] + core))
        for row in range(row_count)
        for j in range(blocks)
        for core in range(2)
    ]
    folded = lax.ppermute(send, ("row", "col"), fold)
    copies = pl.pallas_call(
        spread,
        out_shape=jax.ShapeDtypeStruct((2 * blocks,) + message.shape, jnp.float32),
        in_specs=[vmem, vmem],
        out_specs=vmem,
        compiler_params=params,
    )(message, folded)
    planes = [
        [device(2 * turn + low_bit, 2 * j + core) for low_bit in range(2) for j in range(blocks)]
        for turn in range(turns)
        for core in range(2)
    ]
    plane = lax.all_to_all(copies, ("row", "col"), 0, 0, axis_index_groups=planes, tiled=True)
    tile_count = phase_cov.shape[1] // TILE_ROWS
    cut = jnp.transpose(phase_cov.reshape(col_width, tile_count, TILE_ROWS), (1, 0, 2)).astype(jnp.float32)
    plane, cut = lax.optimization_barrier((plane, cut))
    phase = lax.all_to_all(cut, "col", 0, 0, tiled=True).reshape(col_count * col_width, TILE_ROWS)
    slots = [plane]
    for step in range(1, turns):
        turn_on = [(2 * turn + bit, 2 * ((turn + step) % turns) + bit) for turn in range(turns) for bit in range(2)]
        slots.append(lax.ppermute(plane, "row", turn_on))
    own = jnp.stack(slots)
    other = lax.ppermute(own, "col", [(col, col ^ 1) for col in range(col_count)])
    low, solved = pl.pallas_call(
        block_solve,
        out_shape=[
            jax.ShapeDtypeStruct((rank_width, row_count * block_rows), jnp.bfloat16),
            jax.ShapeDtypeStruct((col_width, rank_width), jnp.float32),
        ],
        in_specs=[vmem, vmem],
        out_specs=[vmem, vmem],
        scratch_shapes=[
            pltpu.VMEM((row_count, rank_width, block_rows), jnp.float32),
            pltpu.VMEM((rank_width, block_rows), jnp.float32),
        ],
        compiler_params=params,
        cost_estimate=pl.CostEstimate(flops=800_000_000, bytes_accessed=3_000_000, transcendentals=0),
    )(own, other)
    basis = pl.pallas_call(
        tile_basis,
        out_shape=jax.ShapeDtypeStruct((TILE_ROWS, rank_width), jnp.float32),
        in_specs=[vmem, vmem],
        out_specs=vmem,
        scratch_shapes=[pltpu.VMEM((rank_width, rank_width), jnp.float32)],
        compiler_params=params,
        cost_estimate=pl.CostEstimate(flops=1_000_000_000, bytes_accessed=3_000_000, transcendentals=0),
    )(low, phase)
    basis = basis.reshape(col_count, TILE_ROWS // col_count, rank_width)
    return (lax.all_to_all(basis, "col", 0, 0, tiled=True), solved)


def solution(mesh):
    in_specs = (P("row", None), P("row", "col"), P("row", None), P("col", "row"))
    out_specs = (P("row", "col", None), P("col", None))
    return jax.shard_map(local, mesh=mesh, in_specs=in_specs, out_specs=out_specs, check_vma=False)
```

```python
import functools

import jax
import jax.numpy as jnp
from jax import lax
from jax.experimental import pallas as pl
from jax.experimental.pallas import tpu as pltpu
from jax.sharding import PartitionSpec as P

TILE_ROWS = 512
PANEL = 32
SUBLANES = 8
TURNS = 4
PLANE_BLOCKS = 7
HIGHEST = lax.Precision.HIGHEST
VMEM_BYTES = 48 * 1024 * 1024


def contract(a, b, da, db):
    return lax.dot_general(a, b, (((da,), (db,)), ((), ())), precision=HIGHEST, preferred_element_type=jnp.float32)


def split(a):
    high = a.astype(jnp.bfloat16)
    return high, (a - high.astype(jnp.float32)).astype(jnp.bfloat16)


def dot3(a, b):
    dot = functools.partial(jnp.dot, preferred_element_type=jnp.float32)
    return dot(a[0], b[0]) + (dot(a[0], b[1]) + dot(a[1], b[0]))


def place_of(block_row, block_col):
    turn = block_row // 2
    count = block_col + block_row % 2 * 2 * turn
    if count < PLANE_BLOCKS:
        return turn, count
    return TURNS - 1 - turn, count - PLANE_BLOCKS + 4 * (TURNS - 1 - turn) + 1


def prepare(right_hbm, factor_hbm, diag_hbm, copies_ref, right, factor, diag, scratch, arrived):
    sources = ((diag_hbm, diag), (factor_hbm, factor), (right_hbm, right))
    copies = [pltpu.make_async_copy(source, target, arrived.at[i]) for i, (source, target) in enumerate(sources)]
    for copy in copies:
        copy.start()
    for copy in copies:
        copy.wait()
    half = factor.shape[0]
    chunk = copies_ref.shape[1] - half
    scaled = contract(factor[...], diag[...], 1, 1)
    scratch[...] = contract(right[...], diag[...], 0, 1)
    rows = scratch[pl.ds(pl.multiple_of(lax.axis_index("col") * chunk, chunk), chunk), :]
    for at in range(copies_ref.shape[0]):
        copies_ref[at, :half] = scaled
        copies_ref[at, half:] = rows


def plane_index(turn, count, last):
    return jnp.minimum(jnp.where(count < 2 * turn, count, count + (last + 1) // 2 - 2 * turn), last)


def pick_excess(plane_ref, send_ref):
    turn = lax.axis_index("row") // 2
    half = send_ref.shape[1]
    for at in range(send_ref.shape[0]):
        send_ref[at] = plane_ref[plane_index(turn, at + PLANE_BLOCKS, plane_ref.shape[0] - 1), :half]


def even_out(plane_ref, got_ref, out_ref):
    turn = lax.axis_index("row") // 2
    places, rows, _ = plane_ref.shape
    half = got_ref.shape[1]
    for at in range(PLANE_BLOCKS):
        held = (turn >= TURNS // 2) | (at <= 4 * turn)
        other = jnp.clip(at - 4 * turn - 1, 0, got_ref.shape[0] - 1)
        own = plane_ref[plane_index(turn, at, places - 1), :half]
        out_ref[at * half : (at + 1) * half] = jnp.where(held, own, got_ref[other])
    start = PLANE_BLOCKS * half
    chunk = rows - half
    for at in range(places):
        out_ref[start + at * chunk : start + (at + 1) * chunk] = plane_ref[at, half:]


def factor_and_invert(work, size):
    shape = (SUBLANES, size)
    lane = lax.broadcasted_iota(jnp.int32, shape, 1)
    sublane = lax.broadcasted_iota(jnp.int32, shape, 0)
    for start in range(0, size, PANEL):
        end = start + PANEL
        groups = [work[at : at + SUBLANES, :] for at in range(start, end, SUBLANES)]
        for g in range(len(groups)):
            first = start + g * SUBLANES
            inside = (lane >= first) & (lane < first + SUBLANES)
            columns = [jnp.broadcast_to(groups[g][:, first + j : first + j + 1], shape) for j in range(SUBLANES)]
            pivot = {(i, j): jnp.broadcast_to(columns[j][i : i + 1, :], shape) for j in range(SUBLANES) for i in range(j, SUBLANES)}
            rows, scales = [], []
            for i in range(SUBLANES):
                row = jnp.broadcast_to(groups[g][i : i + 1, :], shape)
                rows.append(jnp.where(inside, jnp.where(lane == first + i, 1.0, 0.0), row))
            for j in range(SUBLANES):
                scale = lax.rsqrt(pivot[j, j])
                scales.append(scale)
                rows[j] = rows[j] * scale
                for i in range(j + 1, SUBLANES):
                    pivot[i, j] = pivot[i, j] * scale
                for i in range(j + 1, SUBLANES):
                    for k in range(j + 1, i + 1):
                        pivot[i, k] = pivot[i, k] - pivot[i, j] * pivot[k, j]
                    rows[i] = rows[i] - pivot[i, j] * rows[j]
            merged = rows[0]
            for i in range(1, SUBLANES):
                merged = jnp.where(sublane == i, rows[i], merged)
            groups[g] = merged
            for h in range(g + 1, len(groups)):
                left = []
                rest = jnp.where(inside, 0.0, groups[h])
                for j in range(SUBLANES):
                    column = jnp.broadcast_to(groups[h][:, first + j : first + j + 1], shape)
                    for i in range(j):
                        column = column - left[i] * pivot[j, i]
                    left.append(column * scales[j])
                    rest = rest - left[j] * rows[j]
                groups[h] = rest
        panel = jnp.concatenate(groups, axis=0)
        work[start:end, :] = panel
        if end < size:
            row_lane = lax.broadcasted_iota(jnp.int32, (size - end, size), 1)
            rest = jnp.where((row_lane >= start) & (row_lane < end), 0.0, work[end:, :])
            panel_lane = lax.broadcasted_iota(jnp.int32, panel.shape, 1)
            panel_row = lax.broadcasted_iota(jnp.int32, panel.shape, 0) + start
            known = jnp.where((panel_lane <= panel_row) | (panel_lane >= end), panel, 0.0)
            work[end:, :] = rest - contract(panel, known, 0, 0)[end:, :]
    square = (size, size)
    lower = lax.broadcasted_iota(jnp.int32, square, 1) <= lax.broadcasted_iota(jnp.int32, square, 0)
    work[...] = jnp.where(lower, work[...], 0.0)


def block_solve(own_ref, other_ref, low_ref, solved_ref, solved_t, work):
    turns, _, size = own_ref.shape
    blocks = solved_t.shape[0]
    half_rows = size // 2
    chunk = size // (2 * blocks)
    col, row = lax.axis_index("col"), lax.axis_index("row")
    core = col % 2

    def rows_of(turn, half, start, count):
        slot = (row // 2 - turn + turns) % turns
        own, other = own_ref[slot, start : start + count, :], other_ref[slot, start : start + count, :]
        return jnp.where(core == half, own, other)

    current = []
    for i in range(blocks):
        start = PLANE_BLOCKS * half_rows + i % 2 * blocks * chunk
        parts = [rows_of(i // 2, half, start + j * chunk, chunk) for j in range(blocks) for half in range(2)]
        current.append(jnp.concatenate(parts, axis=0))
    for j in range(blocks):
        solved_t[j] = current[j]
        low_ref[:, j * size : (j + 1) * size] = current[j].astype(jnp.bfloat16)
        if j + 1 == blocks:
            break
        solved_pair = split(current[j])
        for i in range(j + 1, blocks):
            turn, slot = place_of(i, j)
            parts = [rows_of(turn, half, slot * half_rows, half_rows) for half in range(2)]
            current[i] = current[i] - dot3(solved_pair, split(jnp.concatenate(parts, axis=0)))
    work[...] = solved_t[col // 2].T
    solved_ref[...] = work[pl.ds(pl.multiple_of(core * half_rows, half_rows), half_rows), :]


def tile_basis(low_ref, phase_ref, basis_ref, work):
    size = low_ref.shape[0]
    phase = phase_ref[...].astype(jnp.bfloat16)
    weighted_t = jnp.dot(low_ref[...], phase, preferred_element_type=jnp.float32)
    weighted = weighted_t.T
    work[...] = contract(weighted_t, weighted_t, 1, 1)
    factor_and_invert(work, size)
    basis_ref[...] = contract(weighted, work[...], 1, 1)


def local(right_side, factor_window, diag_inverse, phase_cov):
    row_count = lax.axis_size("row")
    col_count = lax.axis_size("col")
    block_rows = right_side.shape[0]
    rank_width = right_side.shape[1]
    col_width = factor_window.shape[1]
    chunk = rank_width // col_count
    turns = row_count // 2
    blocks = col_count // 2
    vmem = pl.BlockSpec(memory_space=pltpu.VMEM)
    params = pltpu.CompilerParams(vmem_limit_bytes=VMEM_BYTES)
    piece_rows = col_width + chunk
    copies = pl.pallas_call(
        prepare,
        out_shape=jax.ShapeDtypeStruct((2 * blocks, piece_rows, block_rows), jnp.float32),
        in_specs=[pl.BlockSpec(memory_space=pltpu.HBM)] * 3,
        out_specs=vmem,
        scratch_shapes=[
            pltpu.VMEM(right_side.shape, jnp.float32),
            pltpu.VMEM((col_width, block_rows), jnp.float32),
            pltpu.VMEM(diag_inverse.shape, jnp.float32),
            pltpu.VMEM((rank_width, block_rows), jnp.float32),
            pltpu.SemaphoreType.DMA((3,)),
        ],
        compiler_params=pltpu.CompilerParams(vmem_limit_bytes=64 * 1024 * 1024 - 128 * 1024),
    )(right_side, factor_window.T, diag_inverse)

    def device(row, col):
        return row * col_count + col

    planes = [
        [device(2 * turn + low_bit, 2 * j + core) for low_bit in range(2) for j in range(blocks)]
        for turn in range(turns)
        for core in range(2)
    ]
    plane = lax.all_to_all(copies, ("row", "col"), 0, 0, axis_index_groups=planes, tiled=True)
    tile_count = phase_cov.shape[1] // TILE_ROWS
    cut = jnp.transpose(phase_cov.reshape(col_width, tile_count, TILE_ROWS), (1, 0, 2)).astype(jnp.float32)
    excess = pl.pallas_call(
        pick_excess,
        out_shape=jax.ShapeDtypeStruct((PLANE_BLOCKS - 1, col_width, block_rows), jnp.float32),
        in_specs=[vmem],
        out_specs=vmem,
        compiler_params=params,
    )(plane)
    excess, cut = lax.optimization_barrier((excess, cut))
    phase = lax.all_to_all(cut, "col", 0, 0, tiled=True).reshape(col_count * col_width, TILE_ROWS)
    got = lax.ppermute(excess, "row", [(row, 2 * (turns - 1 - row // 2) + row % 2) for row in range(row_count)])
    plane = pl.pallas_call(
        even_out,
        out_shape=jax.ShapeDtypeStruct((PLANE_BLOCKS * col_width + 2 * blocks * chunk, block_rows), jnp.float32),
        in_specs=[vmem, vmem],
        out_specs=vmem,
        compiler_params=params,
    )(plane, got)
    slots = [plane]
    for step in range(1, turns):
        turn_on = [(2 * turn + bit, 2 * ((turn + step) % turns) + bit) for turn in range(turns) for bit in range(2)]
        slots.append(lax.ppermute(plane, "row", turn_on))
    own = jnp.stack(slots)
    other = lax.ppermute(own, "col", [(col, col ^ 1) for col in range(col_count)])
    low, solved = pl.pallas_call(
        block_solve,
        out_shape=[
            jax.ShapeDtypeStruct((rank_width, row_count * block_rows), jnp.bfloat16),
            jax.ShapeDtypeStruct((col_width, rank_width), jnp.float32),
        ],
        in_specs=[vmem, vmem],
        out_specs=[vmem, vmem],
        scratch_shapes=[
            pltpu.VMEM((row_count, rank_width, block_rows), jnp.float32),
            pltpu.VMEM((rank_width, block_rows), jnp.float32),
        ],
        compiler_params=params,
        cost_estimate=pl.CostEstimate(flops=800_000_000, bytes_accessed=3_000_000, transcendentals=0),
    )(own, other)
    basis = pl.pallas_call(
        tile_basis,
        out_shape=jax.ShapeDtypeStruct((TILE_ROWS, rank_width), jnp.float32),
        in_specs=[vmem, vmem],
        out_specs=vmem,
        scratch_shapes=[pltpu.VMEM((rank_width, rank_width), jnp.float32)],
        compiler_params=params,
        cost_estimate=pl.CostEstimate(flops=1_000_000_000, bytes_accessed=3_000_000, transcendentals=0),
    )(low, phase)
    basis = basis.reshape(col_count, TILE_ROWS // col_count, rank_width)
    return (lax.all_to_all(basis, "col", 0, 0, tiled=True), solved)


def solution(mesh):
    in_specs = (P("row", None), P("row", "col"), P("row", None), P("col", "row"))
    out_specs = (P("row", "col", None), P("col", None))
    return jax.shard_map(local, mesh=mesh, in_specs=in_specs, out_specs=out_specs, check_vma=False)
```

```python
import functools

import jax
import jax.numpy as jnp
from jax import lax
from jax.experimental import pallas as pl
from jax.experimental.pallas import tpu as pltpu
from jax.sharding import PartitionSpec as P

TILE_ROWS = 512
PANEL = 32
SUBLANES = 8
TURNS = 4
PLANE_BLOCKS = 7
HIGHEST = lax.Precision.HIGHEST
VMEM_BYTES = 48 * 1024 * 1024


def contract(a, b, da, db):
    return lax.dot_general(a, b, (((da,), (db,)), ((), ())), precision=HIGHEST, preferred_element_type=jnp.float32)


def split(a):
    high = a.astype(jnp.bfloat16)
    return high, (a - high.astype(jnp.float32)).astype(jnp.bfloat16)


def dot3(a, b):
    dot = functools.partial(jnp.dot, preferred_element_type=jnp.float32)
    return dot(a[0], b[0]) + (dot(a[0], b[1]) + dot(a[1], b[0]))


def place_of(block_row, block_col):
    turn = block_row // 2
    count = block_col + block_row % 2 * 2 * turn
    if count < PLANE_BLOCKS:
        return turn, count
    return TURNS - 1 - turn, count - PLANE_BLOCKS + 4 * (TURNS - 1 - turn) + 1


def prepare(right_hbm, factor_hbm, diag_hbm, copies_ref, right, factor, diag, scratch, arrived):
    sources = ((diag_hbm, diag), (factor_hbm, factor), (right_hbm, right))
    copies = [pltpu.make_async_copy(source, target, arrived.at[i]) for i, (source, target) in enumerate(sources)]
    for copy in copies:
        copy.start()
    for copy in copies:
        copy.wait()
    half = factor.shape[0]
    chunk = copies_ref.shape[1] - half
    scaled = contract(factor[...], diag[...], 1, 1)
    scratch[...] = contract(right[...], diag[...], 0, 1)
    rows = scratch[pl.ds(pl.multiple_of(lax.axis_index("col") * chunk, chunk), chunk), :]
    for at in range(copies_ref.shape[0]):
        copies_ref[at, :half] = scaled
        copies_ref[at, half:] = rows


def plane_index(turn, count, last):
    return jnp.minimum(jnp.where(count < 2 * turn, count, count + (last + 1) // 2 - 2 * turn), last)


def pick_excess(plane_ref, send_ref):
    turn = lax.axis_index("row") // 2
    half = send_ref.shape[1]
    for at in range(send_ref.shape[0]):
        send_ref[at] = plane_ref[plane_index(turn, at + PLANE_BLOCKS, plane_ref.shape[0] - 1), :half]


def even_out(plane_ref, got_ref, out_ref):
    turn = lax.axis_index("row") // 2
    places, rows, _ = plane_ref.shape
    half = got_ref.shape[1]
    for at in range(PLANE_BLOCKS):
        held = (turn >= TURNS // 2) | (at <= 4 * turn)
        other = jnp.clip(at - 4 * turn - 1, 0, got_ref.shape[0] - 1)
        own = plane_ref[plane_index(turn, at, places - 1), :half]
        out_ref[at * half : (at + 1) * half] = jnp.where(held, own, got_ref[other])
    start = PLANE_BLOCKS * half
    chunk = rows - half
    for at in range(places):
        out_ref[start + at * chunk : start + (at + 1) * chunk] = plane_ref[at, half:]


def factor_and_invert(work, size):
    shape = (SUBLANES, size)
    lane = lax.broadcasted_iota(jnp.int32, shape, 1)
    sublane = lax.broadcasted_iota(jnp.int32, shape, 0)
    for start in range(0, size, PANEL):
        end = start + PANEL
        groups = [work[at : at + SUBLANES, :] for at in range(start, end, SUBLANES)]
        for g in range(len(groups)):
            first = start + g * SUBLANES
            inside = (lane >= first) & (lane < first + SUBLANES)
            columns = [jnp.broadcast_to(groups[g][:, first + j : first + j + 1], shape) for j in range(SUBLANES)]
            pivot = {(i, j): jnp.broadcast_to(columns[j][i : i + 1, :], shape) for j in range(SUBLANES) for i in range(j, SUBLANES)}
            rows, scales = [], []
            for i in range(SUBLANES):
                row = jnp.broadcast_to(groups[g][i : i + 1, :], shape)
                rows.append(jnp.where(inside, jnp.where(lane == first + i, 1.0, 0.0), row))
            for j in range(SUBLANES):
                scale = lax.rsqrt(pivot[j, j])
                scales.append(scale)
                rows[j] = rows[j] * scale
                for i in range(j + 1, SUBLANES):
                    pivot[i, j] = pivot[i, j] * scale
                for i in range(j + 1, SUBLANES):
                    for k in range(j + 1, i + 1):
                        pivot[i, k] = pivot[i, k] - pivot[i, j] * pivot[k, j]
                    rows[i] = rows[i] - pivot[i, j] * rows[j]
            merged = rows[0]
            for i in range(1, SUBLANES):
                merged = jnp.where(sublane == i, rows[i], merged)
            groups[g] = merged
            for h in range(g + 1, len(groups)):
                left = []
                rest = jnp.where(inside, 0.0, groups[h])
                for j in range(SUBLANES):
                    column = jnp.broadcast_to(groups[h][:, first + j : first + j + 1], shape)
                    for i in range(j):
                        column = column - left[i] * pivot[j, i]
                    left.append(column * scales[j])
                    rest = rest - left[j] * rows[j]
                groups[h] = rest
        panel = jnp.concatenate(groups, axis=0)
        work[start:end, :] = panel
        if end < size:
            row_lane = lax.broadcasted_iota(jnp.int32, (size - end, size), 1)
            rest = jnp.where((row_lane >= start) & (row_lane < end), 0.0, work[end:, :])
            panel_lane = lax.broadcasted_iota(jnp.int32, panel.shape, 1)
            panel_row = lax.broadcasted_iota(jnp.int32, panel.shape, 0) + start
            known = jnp.where((panel_lane <= panel_row) | (panel_lane >= end), panel, 0.0)
            work[end:, :] = rest - contract(panel, known, 0, 0)[end:, :]
    square = (size, size)
    lower = lax.broadcasted_iota(jnp.int32, square, 1) <= lax.broadcasted_iota(jnp.int32, square, 0)
    work[...] = jnp.where(lower, work[...], 0.0)


def block_solve(own_ref, other_ref, low_ref, solved_ref, solved_t, work):
    turns, _, size = own_ref.shape
    blocks = solved_t.shape[0]
    half_rows = size // 2
    chunk = size // (2 * blocks)
    col, row = lax.axis_index("col"), lax.axis_index("row")
    core = col % 2

    def rows_of(turn, half, start, count):
        slot = (row // 2 - turn + turns) % turns
        own, other = own_ref[slot, start : start + count, :], other_ref[slot, start : start + count, :]
        return jnp.where(core == half, own, other)

    current = []
    for i in range(blocks):
        start = PLANE_BLOCKS * half_rows + i % 2 * blocks * chunk
        parts = [rows_of(i // 2, half, start + j * chunk, chunk) for j in range(blocks) for half in range(2)]
        current.append(jnp.concatenate(parts, axis=0))
    for j in range(blocks):
        solved_t[j] = current[j]
        low_ref[:, j * size : (j + 1) * size] = current[j].astype(jnp.bfloat16)
        if j + 1 == blocks:
            break
        solved_pair = split(current[j])
        for i in range(j + 1, blocks):
            turn, slot = place_of(i, j)
            parts = [rows_of(turn, half, slot * half_rows, half_rows) for half in range(2)]
            current[i] = current[i] - dot3(solved_pair, split(jnp.concatenate(parts, axis=0)))
    work[...] = solved_t[col // 2].T
    solved_ref[...] = work[pl.ds(pl.multiple_of(core * half_rows, half_rows), half_rows), :]


def tile_basis(low_ref, phase_ref, basis_ref, work):
    size = low_ref.shape[0]
    phase = phase_ref[...].astype(jnp.bfloat16)
    weighted_t = jnp.dot(low_ref[...], phase, preferred_element_type=jnp.float32)
    weighted = weighted_t.T
    work[...] = contract(weighted_t, weighted_t, 1, 1)
    factor_and_invert(work, size)
    basis_ref[...] = contract(weighted, work[...], 1, 1)


def local(right_side, factor_window, diag_inverse, phase_cov):
    row_count = lax.axis_size("row")
    col_count = lax.axis_size("col")
    block_rows = right_side.shape[0]
    rank_width = right_side.shape[1]
    col_width = factor_window.shape[1]
    chunk = rank_width // col_count
    turns = row_count // 2
    blocks = col_count // 2
    vmem = pl.BlockSpec(memory_space=pltpu.VMEM)
    params = pltpu.CompilerParams(vmem_limit_bytes=VMEM_BYTES)
    piece_rows = col_width + chunk
    copies = pl.pallas_call(
        prepare,
        out_shape=jax.ShapeDtypeStruct((2 * blocks, piece_rows, block_rows), jnp.float32),
        in_specs=[pl.BlockSpec(memory_space=pltpu.HBM)] * 3,
        out_specs=vmem,
        scratch_shapes=[
            pltpu.VMEM(right_side.shape, jnp.float32),
            pltpu.VMEM((col_width, block_rows), jnp.float32),
            pltpu.VMEM(diag_inverse.shape, jnp.float32),
            pltpu.VMEM((rank_width, block_rows), jnp.float32),
            pltpu.SemaphoreType.DMA((3,)),
        ],
        compiler_params=pltpu.CompilerParams(vmem_limit_bytes=64 * 1024 * 1024 - 128 * 1024),
    )(right_side, factor_window.T, diag_inverse)

    def device(row, col):
        return row * col_count + col

    planes = [
        [device(2 * turn + low_bit, 2 * j + core) for low_bit in range(2) for j in range(blocks)]
        for turn in range(turns)
        for core in range(2)
    ]
    plane = lax.all_to_all(copies, ("row", "col"), 0, 0, axis_index_groups=planes, tiled=True)
    tile_count = phase_cov.shape[1] // TILE_ROWS
    cut = jnp.transpose(phase_cov.reshape(col_width, tile_count, TILE_ROWS), (1, 0, 2)).astype(jnp.float32)
    excess = pl.pallas_call(
        pick_excess,
        out_shape=jax.ShapeDtypeStruct((PLANE_BLOCKS - 1, col_width, block_rows), jnp.float32),
        in_specs=[vmem],
        out_specs=vmem,
        compiler_params=params,
    )(plane)
    excess, cut = lax.optimization_barrier((excess, cut))
    phase = lax.all_to_all(cut, "col", 0, 0, tiled=True).reshape(col_count * col_width, TILE_ROWS)
    got = lax.ppermute(excess, "row", [(row, 2 * (turns - 1 - row // 2) + row % 2) for row in range(row_count)])
    plane = pl.pallas_call(
        even_out,
        out_shape=jax.ShapeDtypeStruct((PLANE_BLOCKS * col_width + 2 * blocks * chunk, block_rows), jnp.float32),
        in_specs=[vmem, vmem],
        out_specs=vmem,
        compiler_params=params,
    )(plane, got)
    slots = [plane]
    for step in range(1, turns):
        turn_on = [(2 * turn + bit, 2 * ((turn + step) % turns) + bit) for turn in range(turns) for bit in range(2)]
        slots.append(lax.ppermute(plane, "row", turn_on))
    own = jnp.stack(slots)
    other = lax.ppermute(own, "col", [(col, col ^ 1) for col in range(col_count)])
    low, solved = pl.pallas_call(
        block_solve,
        out_shape=[
            jax.ShapeDtypeStruct((rank_width, row_count * block_rows), jnp.bfloat16),
            jax.ShapeDtypeStruct((col_width, rank_width), jnp.float32),
        ],
        in_specs=[vmem, vmem],
        out_specs=[vmem, vmem],
        scratch_shapes=[
            pltpu.VMEM((row_count, rank_width, block_rows), jnp.float32),
            pltpu.VMEM((rank_width, block_rows), jnp.float32),
        ],
        compiler_params=params,
        cost_estimate=pl.CostEstimate(flops=2_400_000_000, bytes_accessed=3_000_000, transcendentals=0),
    )(own, other)
    basis = pl.pallas_call(
        tile_basis,
        out_shape=jax.ShapeDtypeStruct((TILE_ROWS, rank_width), jnp.float32),
        in_specs=[vmem, vmem],
        out_specs=vmem,
        scratch_shapes=[pltpu.VMEM((rank_width, rank_width), jnp.float32)],
        compiler_params=params,
        cost_estimate=pl.CostEstimate(flops=1_000_000_000, bytes_accessed=3_000_000, transcendentals=0),
    )(low, phase)
    basis = basis.reshape(col_count, TILE_ROWS // col_count, rank_width)
    return (lax.all_to_all(basis, "col", 0, 0, tiled=True), solved)


def solution(mesh):
    in_specs = (P("row", None), P("row", "col"), P("row", None), P("col", "row"))
    out_specs = (P("row", "col", None), P("col", None))
    return jax.shard_map(local, mesh=mesh, in_specs=in_specs, out_specs=out_specs, check_vma=False)
```

```python
import functools

import jax
import jax.numpy as jnp
from jax import lax
from jax.experimental import pallas as pl
from jax.experimental.pallas import tpu as pltpu
from jax.sharding import PartitionSpec as P

TILE_ROWS = 512
PANEL = 32
SUBLANES = 8
TURNS = 4
PLANE_BLOCKS = 7
HIGHEST = lax.Precision.HIGHEST
VMEM_BYTES = 48 * 1024 * 1024


def contract(a, b, da, db):
    return lax.dot_general(a, b, (((da,), (db,)), ((), ())), precision=HIGHEST, preferred_element_type=jnp.float32)


def split(a):
    high = a.astype(jnp.bfloat16)
    return high, (a - high.astype(jnp.float32)).astype(jnp.bfloat16)


def dot3(a, b):
    dot = functools.partial(jnp.dot, preferred_element_type=jnp.float32)
    return dot(a[0], b[0]) + (dot(a[0], b[1]) + dot(a[1], b[0]))


def place_of(block_row, block_col):
    turn = block_row // 2
    count = block_col + block_row % 2 * 2 * turn
    if count < PLANE_BLOCKS:
        return turn, count
    return TURNS - 1 - turn, count - PLANE_BLOCKS + 4 * (TURNS - 1 - turn) + 1


def prepare(right_hbm, factor_hbm, diag_hbm, copies_ref, right, factor, diag, scratch, arrived):
    sources = ((diag_hbm, diag), (factor_hbm, factor), (right_hbm, right))
    copies = [pltpu.make_async_copy(source, target, arrived.at[i]) for i, (source, target) in enumerate(sources)]
    for copy in copies:
        copy.start()
    for copy in copies:
        copy.wait()
    half = factor.shape[0]
    chunk = copies_ref.shape[1] - half
    scaled = contract(factor[...], diag[...], 1, 1)
    scratch[...] = contract(right[...], diag[...], 0, 1)
    rows = scratch[pl.ds(pl.multiple_of(lax.axis_index("col") * chunk, chunk), chunk), :]
    for at in range(copies_ref.shape[0]):
        copies_ref[at, :half] = scaled
        copies_ref[at, half:] = rows


def plane_index(turn, count, last):
    return jnp.minimum(jnp.where(count < 2 * turn, count, count + (last + 1) // 2 - 2 * turn), last)


def pick_excess(plane_ref, send_ref):
    turn = lax.axis_index("row") // 2
    half = send_ref.shape[1]
    for at in range(send_ref.shape[0]):
        send_ref[at] = plane_ref[plane_index(turn, at + PLANE_BLOCKS, plane_ref.shape[0] - 1), :half]


def even_out(plane_ref, got_ref, out_ref):
    turn = lax.axis_index("row") // 2
    places, rows, _ = plane_ref.shape
    half = got_ref.shape[1]
    for at in range(PLANE_BLOCKS):
        held = (turn >= TURNS // 2) | (at <= 4 * turn)
        other = jnp.clip(at - 4 * turn - 1, 0, got_ref.shape[0] - 1)
        own = plane_ref[plane_index(turn, at, places - 1), :half]
        out_ref[at * half : (at + 1) * half] = jnp.where(held, own, got_ref[other])
    start = PLANE_BLOCKS * half
    chunk = rows - half
    for at in range(places):
        out_ref[start + at * chunk : start + (at + 1) * chunk] = plane_ref[at, half:]


def factor_and_invert(work, size):
    shape = (SUBLANES, size)
    lane = lax.broadcasted_iota(jnp.int32, shape, 1)
    sublane = lax.broadcasted_iota(jnp.int32, shape, 0)
    for start in range(0, size, PANEL):
        end = start + PANEL
        groups = [work[at : at + SUBLANES, :] for at in range(start, end, SUBLANES)]
        for g in range(len(groups)):
            first = start + g * SUBLANES
            inside = (lane >= first) & (lane < first + SUBLANES)
            columns = [jnp.broadcast_to(groups[g][:, first + j : first + j + 1], shape) for j in range(SUBLANES)]
            pivot = {(i, j): jnp.broadcast_to(columns[j][i : i + 1, :], shape) for j in range(SUBLANES) for i in range(j, SUBLANES)}
            rows, scales = [], []
            for i in range(SUBLANES):
                row = jnp.broadcast_to(groups[g][i : i + 1, :], shape)
                rows.append(jnp.where(inside, jnp.where(lane == first + i, 1.0, 0.0), row))
            for j in range(SUBLANES):
                scale = lax.rsqrt(pivot[j, j])
                scales.append(scale)
                rows[j] = rows[j] * scale
                for i in range(j + 1, SUBLANES):
                    pivot[i, j] = pivot[i, j] * scale
                for i in range(j + 1, SUBLANES):
                    for k in range(j + 1, i + 1):
                        pivot[i, k] = pivot[i, k] - pivot[i, j] * pivot[k, j]
                    rows[i] = rows[i] - pivot[i, j] * rows[j]
            merged = rows[0]
            for i in range(1, SUBLANES):
                merged = jnp.where(sublane == i, rows[i], merged)
            groups[g] = merged
            for h in range(g + 1, len(groups)):
                left = []
                rest = jnp.where(inside, 0.0, groups[h])
                for j in range(SUBLANES):
                    column = jnp.broadcast_to(groups[h][:, first + j : first + j + 1], shape)
                    for i in range(j):
                        column = column - left[i] * pivot[j, i]
                    left.append(column * scales[j])
                    rest = rest - left[j] * rows[j]
                groups[h] = rest
        panel = jnp.concatenate(groups, axis=0)
        work[start:end, :] = panel
        if end < size:
            row_lane = lax.broadcasted_iota(jnp.int32, (size - end, size), 1)
            rest = jnp.where((row_lane >= start) & (row_lane < end), 0.0, work[end:, :])
            panel_lane = lax.broadcasted_iota(jnp.int32, panel.shape, 1)
            panel_row = lax.broadcasted_iota(jnp.int32, panel.shape, 0) + start
            known = jnp.where((panel_lane <= panel_row) | (panel_lane >= end), panel, 0.0)
            work[end:, :] = rest - contract(panel, known, 0, 0)[end:, :]
    square = (size, size)
    lower = lax.broadcasted_iota(jnp.int32, square, 1) <= lax.broadcasted_iota(jnp.int32, square, 0)
    work[...] = jnp.where(lower, work[...], 0.0)


def cut_tiles(cov_ref, keep_ref, *give_refs):
    count, _, width = keep_ref.shape
    core = lax.axis_index("col") % 2
    for at in range(count):
        part = give_refs[0].shape[0]
        for out_ref, place, there in ((keep_ref, at, core), (give_refs[at // part], at % part, 1 - core)):
            tile = 2 * at + there
            out_ref[place] = cov_ref[:, pl.ds(pl.multiple_of(tile * width, width), width)].astype(jnp.float32)


def pair_rows(keep_ref, *refs):
    rows = keep_ref.shape[1]
    first = lax.axis_index("col") % 2 == 0
    got_refs, out_ref = refs[:-1], refs[-1]
    part = got_refs[0].shape[0]
    for at in range(keep_ref.shape[0]):
        keep, got = keep_ref[at], got_refs[at // part][at % part]
        out_ref[at, :rows] = jnp.where(first, keep, got)
        out_ref[at, rows:] = jnp.where(first, got, keep)


def block_solve(own_ref, other_ref, low_ref, solved_ref, solved_t, work):
    turns, _, size = own_ref.shape
    blocks = solved_t.shape[0]
    half_rows = size // 2
    chunk = size // (2 * blocks)
    col, row = lax.axis_index("col"), lax.axis_index("row")
    core = col % 2

    def rows_of(turn, half, start, count):
        slot = (row // 2 - turn + turns) % turns
        own, other = own_ref[slot, start : start + count, :], other_ref[slot, start : start + count, :]
        return jnp.where(core == half, own, other)

    current = []
    for i in range(blocks):
        start = PLANE_BLOCKS * half_rows + i % 2 * blocks * chunk
        parts = [rows_of(i // 2, half, start + j * chunk, chunk) for j in range(blocks) for half in range(2)]
        current.append(jnp.concatenate(parts, axis=0))
    for j in range(blocks):
        solved_t[j] = current[j]
        low_ref[:, j * size : (j + 1) * size] = current[j].astype(jnp.bfloat16)
        if j + 1 == blocks:
            break
        solved_pair = split(current[j])
        for i in range(j + 1, blocks):
            turn, slot = place_of(i, j)
            parts = [rows_of(turn, half, slot * half_rows, half_rows) for half in range(2)]
            current[i] = current[i] - dot3(solved_pair, split(jnp.concatenate(parts, axis=0)))
    work[...] = solved_t[col // 2].T
    solved_ref[...] = work[pl.ds(pl.multiple_of(core * half_rows, half_rows), half_rows), :]


def tile_basis(low_ref, phase_ref, basis_ref, work):
    size = low_ref.shape[0]
    phase = phase_ref[...].astype(jnp.bfloat16)
    weighted_t = jnp.dot(low_ref[...], phase, preferred_element_type=jnp.float32)
    weighted = weighted_t.T
    work[...] = contract(weighted_t, weighted_t, 1, 1)
    factor_and_invert(work, size)
    basis_ref[...] = contract(weighted, work[...], 1, 1)


def local(right_side, factor_window, diag_inverse, phase_cov):
    row_count = lax.axis_size("row")
    col_count = lax.axis_size("col")
    block_rows = right_side.shape[0]
    rank_width = right_side.shape[1]
    col_width = factor_window.shape[1]
    chunk = rank_width // col_count
    turns = row_count // 2
    blocks = col_count // 2
    vmem = pl.BlockSpec(memory_space=pltpu.VMEM)
    params = pltpu.CompilerParams(vmem_limit_bytes=VMEM_BYTES)
    piece_rows = col_width + chunk
    copies = pl.pallas_call(
        prepare,
        out_shape=jax.ShapeDtypeStruct((2 * blocks, piece_rows, block_rows), jnp.float32),
        in_specs=[pl.BlockSpec(memory_space=pltpu.HBM)] * 3,
        out_specs=vmem,
        scratch_shapes=[
            pltpu.VMEM(right_side.shape, jnp.float32),
            pltpu.VMEM((col_width, block_rows), jnp.float32),
            pltpu.VMEM(diag_inverse.shape, jnp.float32),
            pltpu.VMEM((rank_width, block_rows), jnp.float32),
            pltpu.SemaphoreType.DMA((3,)),
        ],
        compiler_params=pltpu.CompilerParams(vmem_limit_bytes=64 * 1024 * 1024 - 128 * 1024),
    )(right_side, factor_window.T, diag_inverse)

    def device(row, col):
        return row * col_count + col

    planes = [
        [device(2 * turn + low_bit, 2 * j + core) for low_bit in range(2) for j in range(blocks)]
        for turn in range(turns)
        for core in range(2)
    ]
    copies, cov = lax.optimization_barrier((copies, phase_cov))
    plane = lax.all_to_all(copies, ("row", "col"), 0, 0, axis_index_groups=planes, tiled=True)
    cores = [(col, col ^ 1) for col in range(col_count)]
    cut_shapes = [jax.ShapeDtypeStruct((blocks // part, col_width, TILE_ROWS), jnp.float32) for part in (1,) + (2,) * 2]
    keep, *gives = pl.pallas_call(
        cut_tiles,
        out_shape=cut_shapes,
        in_specs=[vmem],
        out_specs=[vmem] * len(cut_shapes),
        compiler_params=params,
    )(cov)
    cut = pl.pallas_call(
        pair_rows,
        out_shape=jax.ShapeDtypeStruct((blocks, 2 * col_width, TILE_ROWS), jnp.float32),
        in_specs=[vmem] * len(cut_shapes),
        out_specs=vmem,
        compiler_params=params,
    )(keep, *[lax.ppermute(give, "col", cores) for give in gives])
    plane, cut = lax.optimization_barrier((plane, cut))
    excess = pl.pallas_call(
        pick_excess,
        out_shape=jax.ShapeDtypeStruct((PLANE_BLOCKS - 1, col_width, block_rows), jnp.float32),
        in_specs=[vmem],
        out_specs=vmem,
        compiler_params=params,
    )(plane)
    excess, cut = lax.optimization_barrier((excess, cut))
    groups = [[2 * j + core for j in range(blocks)] for core in range(2)]
    phase = lax.all_to_all(cut, "col", 0, 0, axis_index_groups=groups, tiled=True).reshape(col_count * col_width, TILE_ROWS)
    got = lax.ppermute(excess, "row", [(row, 2 * (turns - 1 - row // 2) + row % 2) for row in range(row_count)])
    plane = pl.pallas_call(
        even_out,
        out_shape=jax.ShapeDtypeStruct((PLANE_BLOCKS * col_width + 2 * blocks * chunk, block_rows), jnp.float32),
        in_specs=[vmem, vmem],
        out_specs=vmem,
        compiler_params=params,
    )(plane, got)
    slots = [plane]
    for step in range(1, turns):
        turn_on = [(2 * turn + bit, 2 * ((turn + step) % turns) + bit) for turn in range(turns) for bit in range(2)]
        slots.append(lax.ppermute(plane, "row", turn_on))
    own = jnp.stack(slots)
    other = lax.ppermute(own, "col", cores)
    low, solved = pl.pallas_call(
        block_solve,
        out_shape=[
            jax.ShapeDtypeStruct((rank_width, row_count * block_rows), jnp.bfloat16),
            jax.ShapeDtypeStruct((col_width, rank_width), jnp.float32),
        ],
        in_specs=[vmem, vmem],
        out_specs=[vmem, vmem],
        scratch_shapes=[
            pltpu.VMEM((row_count, rank_width, block_rows), jnp.float32),
            pltpu.VMEM((rank_width, block_rows), jnp.float32),
        ],
        compiler_params=params,
        cost_estimate=pl.CostEstimate(flops=1_600_000_000, bytes_accessed=3_000_000, transcendentals=0),
    )(own, other)
    basis = pl.pallas_call(
        tile_basis,
        out_shape=jax.ShapeDtypeStruct((TILE_ROWS, rank_width), jnp.float32),
        in_specs=[vmem, vmem],
        out_specs=vmem,
        scratch_shapes=[pltpu.VMEM((rank_width, rank_width), jnp.float32)],
        compiler_params=params,
        cost_estimate=pl.CostEstimate(flops=1_000_000_000, bytes_accessed=3_000_000, transcendentals=0),
    )(low, phase)
    basis = basis.reshape(col_count, TILE_ROWS // col_count, rank_width)
    return (lax.all_to_all(basis, "col", 0, 0, tiled=True), solved)


def solution(mesh):
    in_specs = (P("row", None), P("row", "col"), P("row", None), P("col", "row"))
    out_specs = (P("row", "col", None), P("col", None))
    return jax.shard_map(local, mesh=mesh, in_specs=in_specs, out_specs=out_specs, check_vma=False)
```

```python
import functools

import jax
import jax.numpy as jnp
from jax import lax
from jax.experimental import pallas as pl
from jax.experimental.pallas import tpu as pltpu
from jax.sharding import PartitionSpec as P

TILE_ROWS = 512
PANEL = 32
SUBLANES = 8
TURNS = 4
PLANE_BLOCKS = 7
HIGHEST = lax.Precision.HIGHEST
VMEM_BYTES = 48 * 1024 * 1024


def contract(a, b, da, db):
    return lax.dot_general(a, b, (((da,), (db,)), ((), ())), precision=HIGHEST, preferred_element_type=jnp.float32)


def split(a):
    high = a.astype(jnp.bfloat16)
    return high, (a - high.astype(jnp.float32)).astype(jnp.bfloat16)


def dot3(a, b):
    dot = functools.partial(jnp.dot, preferred_element_type=jnp.float32)
    return dot(a[0], b[0]) + (dot(a[0], b[1]) + dot(a[1], b[0]))


def place_of(block_row, block_col):
    turn = block_row // 2
    count = block_col + block_row % 2 * 2 * turn
    if count < PLANE_BLOCKS:
        return turn, count
    return TURNS - 1 - turn, count - PLANE_BLOCKS + 4 * (TURNS - 1 - turn) + 1


def prepare(right_hbm, factor_hbm, diag_hbm, copies_ref, side_ref, right, factor, diag, scratch, arrived):
    sources = ((diag_hbm, diag), (factor_hbm, factor), (right_hbm, right))
    copies = [pltpu.make_async_copy(source, target, arrived.at[i]) for i, (source, target) in enumerate(sources)]
    for copy in copies:
        copy.start()
    for copy in copies:
        copy.wait()
    scaled = contract(factor[...], diag[...], 1, 1)
    for at in range(copies_ref.shape[0]):
        copies_ref[at] = scaled
    scratch[...] = contract(right[...], diag[...], 0, 1)
    half = side_ref.shape[0]
    side_ref[...] = scratch[pl.ds(pl.multiple_of(lax.axis_index("col") % 2 * half, half), half), :]


def plane_index(turn, count, last):
    return jnp.minimum(jnp.where(count < 2 * turn, count, count + (last + 1) // 2 - 2 * turn), last)


def pick_excess(plane_ref, send_ref):
    turn = lax.axis_index("row") // 2
    for at in range(send_ref.shape[0]):
        send_ref[at] = plane_ref[plane_index(turn, at + PLANE_BLOCKS, plane_ref.shape[0] - 1)]


def even_out(plane_ref, got_ref, side_ref, beside_ref, out_ref):
    row = lax.axis_index("row")
    turn = row // 2
    places, half, _ = plane_ref.shape
    for at in range(PLANE_BLOCKS):
        held = (turn >= TURNS // 2) | (at <= 4 * turn)
        other = jnp.clip(at - 4 * turn - 1, 0, got_ref.shape[0] - 1)
        own = plane_ref[plane_index(turn, at, places - 1)]
        out_ref[at * half : (at + 1) * half] = jnp.where(held, own, got_ref[other])
    for low_bit in range(2):
        start = (PLANE_BLOCKS + low_bit) * half
        out_ref[start : start + half] = jnp.where(row % 2 == low_bit, side_ref[...], beside_ref[...])


def factor_and_invert(work, size):
    shape = (SUBLANES, size)
    lane = lax.broadcasted_iota(jnp.int32, shape, 1)
    sublane = lax.broadcasted_iota(jnp.int32, shape, 0)
    for start in range(0, size, PANEL):
        end = start + PANEL
        groups = [work[at : at + SUBLANES, :] for at in range(start, end, SUBLANES)]
        for g in range(len(groups)):
            first = start + g * SUBLANES
            inside = (lane >= first) & (lane < first + SUBLANES)
            columns = [jnp.broadcast_to(groups[g][:, first + j : first + j + 1], shape) for j in range(SUBLANES)]
            pivot = {(i, j): jnp.broadcast_to(columns[j][i : i + 1, :], shape) for j in range(SUBLANES) for i in range(j, SUBLANES)}
            rows, scales = [], []
            for i in range(SUBLANES):
                row = jnp.broadcast_to(groups[g][i : i + 1, :], shape)
                rows.append(jnp.where(inside, jnp.where(lane == first + i, 1.0, 0.0), row))
            for j in range(SUBLANES):
                scale = lax.rsqrt(pivot[j, j])
                scales.append(scale)
                rows[j] = rows[j] * scale
                for i in range(j + 1, SUBLANES):
                    pivot[i, j] = pivot[i, j] * scale
                for i in range(j + 1, SUBLANES):
                    for k in range(j + 1, i + 1):
                        pivot[i, k] = pivot[i, k] - pivot[i, j] * pivot[k, j]
                    rows[i] = rows[i] - pivot[i, j] * rows[j]
            merged = rows[0]
            for i in range(1, SUBLANES):
                merged = jnp.where(sublane == i, rows[i], merged)
            groups[g] = merged
            for h in range(g + 1, len(groups)):
                left = []
                rest = jnp.where(inside, 0.0, groups[h])
                for j in range(SUBLANES):
                    column = jnp.broadcast_to(groups[h][:, first + j : first + j + 1], shape)
                    for i in range(j):
                        column = column - left[i] * pivot[j, i]
                    left.append(column * scales[j])
                    rest = rest - left[j] * rows[j]
                groups[h] = rest
        panel = jnp.concatenate(groups, axis=0)
        work[start:end, :] = panel
        if end < size:
            row_lane = lax.broadcasted_iota(jnp.int32, (size - end, size), 1)
            rest = jnp.where((row_lane >= start) & (row_lane < end), 0.0, work[end:, :])
            panel_lane = lax.broadcasted_iota(jnp.int32, panel.shape, 1)
            panel_row = lax.broadcasted_iota(jnp.int32, panel.shape, 0) + start
            known = jnp.where((panel_lane <= panel_row) | (panel_lane >= end), panel, 0.0)
            work[end:, :] = rest - contract(panel, known, 0, 0)[end:, :]
    square = (size, size)
    lower = lax.broadcasted_iota(jnp.int32, square, 1) <= lax.broadcasted_iota(jnp.int32, square, 0)
    work[...] = jnp.where(lower, work[...], 0.0)


def cut_tiles(cov_ref, keep_ref, *give_refs):
    count, _, width = keep_ref.shape
    core = lax.axis_index("col") % 2
    for at in range(count):
        part = give_refs[0].shape[0]
        for out_ref, place, there in ((keep_ref, at, core), (give_refs[at // part], at % part, 1 - core)):
            tile = 2 * at + there
            out_ref[place] = cov_ref[:, pl.ds(pl.multiple_of(tile * width, width), width)].astype(jnp.float32)


def pair_rows(keep_ref, *refs):
    rows = keep_ref.shape[1]
    first = lax.axis_index("col") % 2 == 0
    got_refs, out_ref = refs[:-1], refs[-1]
    part = got_refs[0].shape[0]
    for at in range(keep_ref.shape[0]):
        keep, got = keep_ref[at], got_refs[at // part][at % part]
        out_ref[at, :rows] = jnp.where(first, keep, got)
        out_ref[at, rows:] = jnp.where(first, got, keep)


def block_solve(own_ref, other_ref, low_ref, solved_ref, solved_t, work):
    turns, _, size = own_ref.shape
    blocks = solved_t.shape[0]
    half_rows = size // 2
    col, row = lax.axis_index("col"), lax.axis_index("row")
    core = col % 2

    def rows_of(turn, half, start, count):
        slot = (row // 2 - turn + turns) % turns
        own, other = own_ref[slot, start : start + count, :], other_ref[slot, start : start + count, :]
        return jnp.where(core == half, own, other)

    current = []
    for i in range(blocks):
        start = (PLANE_BLOCKS + i % 2) * half_rows
        parts = [rows_of(i // 2, half, start, half_rows) for half in range(2)]
        current.append(jnp.concatenate(parts, axis=0))
    for j in range(blocks):
        solved_t[j] = current[j]
        low_ref[:, j * size : (j + 1) * size] = current[j].astype(jnp.bfloat16)
        if j + 1 == blocks:
            break
        solved_pair = split(current[j])
        for i in range(j + 1, blocks):
            turn, slot = place_of(i, j)
            parts = [rows_of(turn, half, slot * half_rows, half_rows) for half in range(2)]
            current[i] = current[i] - dot3(solved_pair, split(jnp.concatenate(parts, axis=0)))
    work[...] = solved_t[col // 2].T
    solved_ref[...] = work[pl.ds(pl.multiple_of(core * half_rows, half_rows), half_rows), :]


def tile_basis(low_ref, phase_ref, basis_ref, work):
    size = low_ref.shape[0]
    phase = phase_ref[...].astype(jnp.bfloat16)
    weighted_t = jnp.dot(low_ref[...], phase, preferred_element_type=jnp.float32)
    weighted = weighted_t.T
    work[...] = contract(weighted_t, weighted_t, 1, 1)
    factor_and_invert(work, size)
    basis_ref[...] = contract(weighted, work[...], 1, 1)


def local(right_side, factor_window, diag_inverse, phase_cov):
    row_count = lax.axis_size("row")
    col_count = lax.axis_size("col")
    block_rows = right_side.shape[0]
    rank_width = right_side.shape[1]
    col_width = factor_window.shape[1]
    turns = row_count // 2
    blocks = col_count // 2
    vmem = pl.BlockSpec(memory_space=pltpu.VMEM)
    params = pltpu.CompilerParams(vmem_limit_bytes=VMEM_BYTES)
    half_rank = rank_width // 2
    copies, side = pl.pallas_call(
        prepare,
        out_shape=[
            jax.ShapeDtypeStruct((2 * blocks, col_width, block_rows), jnp.float32),
            jax.ShapeDtypeStruct((half_rank, block_rows), jnp.float32),
        ],
        in_specs=[pl.BlockSpec(memory_space=pltpu.HBM)] * 3,
        out_specs=[vmem, vmem],
        scratch_shapes=[
            pltpu.VMEM(right_side.shape, jnp.float32),
            pltpu.VMEM((col_width, block_rows), jnp.float32),
            pltpu.VMEM(diag_inverse.shape, jnp.float32),
            pltpu.VMEM((rank_width, block_rows), jnp.float32),
            pltpu.SemaphoreType.DMA((3,)),
        ],
        compiler_params=pltpu.CompilerParams(vmem_limit_bytes=64 * 1024 * 1024 - 128 * 1024),
    )(right_side, factor_window.T, diag_inverse)

    def device(row, col):
        return row * col_count + col

    planes = [
        [device(2 * turn + low_bit, 2 * j + core) for low_bit in range(2) for j in range(blocks)]
        for turn in range(turns)
        for core in range(2)
    ]
    copies, cov = lax.optimization_barrier((copies, phase_cov))
    plane = lax.all_to_all(copies, ("row", "col"), 0, 0, axis_index_groups=planes, tiled=True)
    cores = [(col, col ^ 1) for col in range(col_count)]
    cut_shapes = [jax.ShapeDtypeStruct((blocks // part, col_width, TILE_ROWS), jnp.float32) for part in (1,) + (4,) * 4]
    keep, *gives = pl.pallas_call(
        cut_tiles,
        out_shape=cut_shapes,
        in_specs=[vmem],
        out_specs=[vmem] * len(cut_shapes),
        compiler_params=params,
    )(cov)
    cut = pl.pallas_call(
        pair_rows,
        out_shape=jax.ShapeDtypeStruct((blocks, 2 * col_width, TILE_ROWS), jnp.float32),
        in_specs=[vmem] * len(cut_shapes),
        out_specs=vmem,
        compiler_params=params,
    )(keep, *[lax.ppermute(give, "col", cores) for give in gives])
    beside = lax.ppermute(side, "row", [(row, row ^ 1) for row in range(row_count)])
    plane, cut, beside = lax.optimization_barrier((plane, cut, beside))
    excess = pl.pallas_call(
        pick_excess,
        out_shape=jax.ShapeDtypeStruct((PLANE_BLOCKS - 1, col_width, block_rows), jnp.float32),
        in_specs=[vmem],
        out_specs=vmem,
        compiler_params=params,
    )(plane)
    excess, cut = lax.optimization_barrier((excess, cut))
    groups = [[2 * j + core for j in range(blocks)] for core in range(2)]
    phase = lax.all_to_all(cut, "col", 0, 0, axis_index_groups=groups, tiled=True).reshape(col_count * col_width, TILE_ROWS)
    got = lax.ppermute(excess, "row", [(row, 2 * (turns - 1 - row // 2) + row % 2) for row in range(row_count)])
    plane = pl.pallas_call(
        even_out,
        out_shape=jax.ShapeDtypeStruct(((PLANE_BLOCKS + 2) * col_width, block_rows), jnp.float32),
        in_specs=[vmem] * 4,
        out_specs=vmem,
        compiler_params=params,
    )(plane, got, side, beside)
    slots = [plane]
    for step in range(1, turns):
        turn_on = [(2 * turn + bit, 2 * ((turn + step) % turns) + bit) for turn in range(turns) for bit in range(2)]
        slots.append(lax.ppermute(plane, "row", turn_on))
    own = jnp.stack(slots)
    other = lax.ppermute(own, "col", cores)
    low, solved = pl.pallas_call(
        block_solve,
        out_shape=[
            jax.ShapeDtypeStruct((rank_width, row_count * block_rows), jnp.bfloat16),
            jax.ShapeDtypeStruct((col_width, rank_width), jnp.float32),
        ],
        in_specs=[vmem, vmem],
        out_specs=[vmem, vmem],
        scratch_shapes=[
            pltpu.VMEM((row_count, rank_width, block_rows), jnp.float32),
            pltpu.VMEM((rank_width, block_rows), jnp.float32),
        ],
        compiler_params=params,
        cost_estimate=pl.CostEstimate(flops=1_600_000_000, bytes_accessed=3_000_000, transcendentals=0),
    )(own, other)
    basis = pl.pallas_call(
        tile_basis,
        out_shape=jax.ShapeDtypeStruct((TILE_ROWS, rank_width), jnp.float32),
        in_specs=[vmem, vmem],
        out_specs=vmem,
        scratch_shapes=[pltpu.VMEM((rank_width, rank_width), jnp.float32)],
        compiler_params=params,
        cost_estimate=pl.CostEstimate(flops=1_000_000_000, bytes_accessed=3_000_000, transcendentals=0),
    )(low, phase)
    basis = basis.reshape(col_count, TILE_ROWS // col_count, rank_width)
    return (lax.all_to_all(basis, "col", 0, 0, tiled=True), solved)


def solution(mesh):
    in_specs = (P("row", None), P("row", "col"), P("row", None), P("col", "row"))
    out_specs = (P("row", "col", None), P("col", None))
    return jax.shard_map(local, mesh=mesh, in_specs=in_specs, out_specs=out_specs, check_vma=False)
```

```python
import functools

import jax
import jax.numpy as jnp
from jax import lax
from jax.experimental import pallas as pl
from jax.experimental.pallas import tpu as pltpu
from jax.sharding import PartitionSpec as P

TILE_ROWS = 512
PANEL = 64
SUBLANES = 8
TURNS = 4
PLANE_BLOCKS = 7
CORE_PARTS = (3, 3, 2)
HIGHEST = lax.Precision.HIGHEST
VMEM_BYTES = 48 * 1024 * 1024


def contract(a, b, da, db):
    return lax.dot_general(a, b, (((da,), (db,)), ((), ())), precision=HIGHEST, preferred_element_type=jnp.float32)


def split(a):
    high = a.astype(jnp.bfloat16)
    return high, (a - high.astype(jnp.float32)).astype(jnp.bfloat16)


def dot3(a, b):
    dot = functools.partial(jnp.dot, preferred_element_type=jnp.float32)
    return dot(a[0], b[0]) + (dot(a[0], b[1]) + dot(a[1], b[0]))


def place_of(block_row, block_col):
    turn = block_row // 2
    count = block_col + block_row % 2 * 2 * turn
    if count < PLANE_BLOCKS:
        return turn, count
    return TURNS - 1 - turn, count - PLANE_BLOCKS + 4 * (TURNS - 1 - turn) + 1


def prepare(right_hbm, factor_hbm, diag_hbm, copies_ref, side_ref, right, factor, diag, scratch, arrived):
    sources = ((diag_hbm, diag), (factor_hbm, factor), (right_hbm, right))
    copies = [pltpu.make_async_copy(source, target, arrived.at[i]) for i, (source, target) in enumerate(sources)]
    for copy in copies:
        copy.start()
    for copy in copies:
        copy.wait()
    scaled = contract(factor[...], diag[...], 1, 1)
    for at in range(copies_ref.shape[0]):
        copies_ref[at] = scaled
    scratch[...] = contract(right[...], diag[...], 0, 1)
    half = side_ref.shape[0]
    side_ref[...] = scratch[pl.ds(pl.multiple_of(lax.axis_index("col") % 2 * half, half), half), :]


def plane_index(turn, count, last):
    return jnp.minimum(jnp.where(count < 2 * turn, count, count + (last + 1) // 2 - 2 * turn), last)


def pick_excess(plane_ref, send_ref):
    turn = lax.axis_index("row") // 2
    for at in range(send_ref.shape[0]):
        send_ref[at] = plane_ref[plane_index(turn, at + PLANE_BLOCKS, plane_ref.shape[0] - 1)]


def even_out(plane_ref, got_ref, side_ref, beside_ref, out_ref):
    row = lax.axis_index("row")
    turn = row // 2
    places, half, _ = plane_ref.shape
    for at in range(PLANE_BLOCKS):
        held = (turn >= TURNS // 2) | (at <= 4 * turn)
        other = jnp.clip(at - 4 * turn - 1, 0, got_ref.shape[0] - 1)
        own = plane_ref[plane_index(turn, at, places - 1)]
        out_ref[at * half : (at + 1) * half] = jnp.where(held, own, got_ref[other])
    for low_bit in range(2):
        start = (PLANE_BLOCKS + low_bit) * half
        out_ref[start : start + half] = jnp.where(row % 2 == low_bit, side_ref[...], beside_ref[...])


def factor_and_invert(work, size):
    shape = (SUBLANES, size)
    lane = lax.broadcasted_iota(jnp.int32, shape, 1)
    sublane = lax.broadcasted_iota(jnp.int32, shape, 0)
    for start in range(0, size, PANEL):
        end = start + PANEL
        groups = [work[at : at + SUBLANES, :] for at in range(start, end, SUBLANES)]
        for g in range(len(groups)):
            first = start + g * SUBLANES
            inside = (lane >= first) & (lane < first + SUBLANES)
            columns = [jnp.broadcast_to(groups[g][:, first + j : first + j + 1], shape) for j in range(SUBLANES)]
            pivot = {(i, j): jnp.broadcast_to(columns[j][i : i + 1, :], shape) for j in range(SUBLANES) for i in range(j, SUBLANES)}
            rows, scales = [], []
            for i in range(SUBLANES):
                row = jnp.broadcast_to(groups[g][i : i + 1, :], shape)
                rows.append(jnp.where(inside, jnp.where(lane == first + i, 1.0, 0.0), row))
            for j in range(SUBLANES):
                scale = lax.rsqrt(pivot[j, j])
                scales.append(scale)
                rows[j] = rows[j] * scale
                for i in range(j + 1, SUBLANES):
                    pivot[i, j] = pivot[i, j] * scale
                for i in range(j + 1, SUBLANES):
                    for k in range(j + 1, i + 1):
                        pivot[i, k] = pivot[i, k] - pivot[i, j] * pivot[k, j]
                    rows[i] = rows[i] - pivot[i, j] * rows[j]
            merged = rows[0]
            for i in range(1, SUBLANES):
                merged = jnp.where(sublane == i, rows[i], merged)
            groups[g] = merged
            for h in range(g + 1, len(groups)):
                left = []
                rest = jnp.where(inside, 0.0, groups[h])
                for j in range(SUBLANES):
                    column = jnp.broadcast_to(groups[h][:, first + j : first + j + 1], shape)
                    for i in range(j):
                        column = column - left[i] * pivot[j, i]
                    left.append(column * scales[j])
                    rest = rest - left[j] * rows[j]
                groups[h] = rest
        panel = jnp.concatenate(groups, axis=0)
        work[start:end, :] = panel
        if end < size:
            row_lane = lax.broadcasted_iota(jnp.int32, (size - end, size), 1)
            rest = jnp.where((row_lane >= start) & (row_lane < end), 0.0, work[end:, :])
            panel_lane = lax.broadcasted_iota(jnp.int32, panel.shape, 1)
            panel_row = lax.broadcasted_iota(jnp.int32, panel.shape, 0) + start
            known = jnp.where((panel_lane <= panel_row) | (panel_lane >= end), panel, 0.0)
            work[end:, :] = rest - contract(panel, known, 0, 0)[end:, :]
    square = (size, size)
    lower = lax.broadcasted_iota(jnp.int32, square, 1) <= lax.broadcasted_iota(jnp.int32, square, 0)
    work[...] = jnp.where(lower, work[...], 0.0)


def cut_tiles(cov_ref, keep_ref, *give_refs):
    count, _, width = keep_ref.shape
    core = lax.axis_index("col") % 2
    for at in range(count):
        part = give_refs[0].shape[0]
        for out_ref, place, there in ((keep_ref, at, core), (give_refs[at // part], at % part, 1 - core)):
            tile = 2 * at + there
            out_ref[place] = cov_ref[:, pl.ds(pl.multiple_of(tile * width, width), width)].astype(jnp.float32)


def pair_rows(keep_ref, *refs):
    rows = keep_ref.shape[1]
    first = lax.axis_index("col") % 2 == 0
    got_refs, out_ref = refs[:-1], refs[-1]
    part = got_refs[0].shape[0]
    for at in range(keep_ref.shape[0]):
        keep, got = keep_ref[at], got_refs[at // part][at % part]
        out_ref[at, :rows] = jnp.where(first, keep, got)
        out_ref[at, rows:] = jnp.where(first, got, keep)


def block_solve(own_ref, other_ref, low_ref, solved_ref, solved_t, work):
    turns, _, size = own_ref.shape
    blocks = solved_t.shape[0]
    half_rows = size // 2
    col, row = lax.axis_index("col"), lax.axis_index("row")
    core = col % 2

    def rows_of(turn, half, start, count):
        slot = (row // 2 - turn + turns) % turns
        own, other = own_ref[slot, start : start + count, :], other_ref[slot, start : start + count, :]
        return jnp.where(core == half, own, other)

    current = []
    for i in range(blocks):
        start = (PLANE_BLOCKS + i % 2) * half_rows
        parts = [rows_of(i // 2, half, start, half_rows) for half in range(2)]
        current.append(jnp.concatenate(parts, axis=0))
    for j in range(blocks):
        solved_t[j] = current[j]
        low_ref[:, j * size : (j + 1) * size] = current[j].astype(jnp.bfloat16)
        if j + 1 == blocks:
            break
        solved_pair = split(current[j])
        for i in range(j + 1, blocks):
            turn, slot = place_of(i, j)
            parts = [rows_of(turn, half, slot * half_rows, half_rows) for half in range(2)]
            current[i] = current[i] - dot3(solved_pair, split(jnp.concatenate(parts, axis=0)))
    work[...] = solved_t[col // 2].T
    solved_ref[...] = work[pl.ds(pl.multiple_of(core * half_rows, half_rows), half_rows), :]


def tile_basis(low_ref, phase_ref, basis_ref, work):
    size = low_ref.shape[0]
    phase = phase_ref[...].astype(jnp.bfloat16)
    weighted_t = jnp.dot(low_ref[...], phase, preferred_element_type=jnp.float32)
    weighted = weighted_t.T
    work[...] = contract(weighted_t, weighted_t, 1, 1)
    factor_and_invert(work, size)
    basis_ref[...] = contract(weighted, work[...], 1, 1)


def local(right_side, factor_window, diag_inverse, phase_cov):
    row_count = lax.axis_size("row")
    col_count = lax.axis_size("col")
    block_rows = right_side.shape[0]
    rank_width = right_side.shape[1]
    col_width = factor_window.shape[1]
    turns = row_count // 2
    blocks = col_count // 2
    vmem = pl.BlockSpec(memory_space=pltpu.VMEM)
    params = pltpu.CompilerParams(vmem_limit_bytes=VMEM_BYTES)
    half_rank = rank_width // 2
    copies, side = pl.pallas_call(
        prepare,
        out_shape=[
            jax.ShapeDtypeStruct((2 * blocks, col_width, block_rows), jnp.float32),
            jax.ShapeDtypeStruct((half_rank, block_rows), jnp.float32),
        ],
        in_specs=[pl.BlockSpec(memory_space=pltpu.HBM)] * 3,
        out_specs=[vmem, vmem],
        scratch_shapes=[
            pltpu.VMEM(right_side.shape, jnp.float32),
            pltpu.VMEM((col_width, block_rows), jnp.float32),
            pltpu.VMEM(diag_inverse.shape, jnp.float32),
            pltpu.VMEM((rank_width, block_rows), jnp.float32),
            pltpu.SemaphoreType.DMA((3,)),
        ],
        compiler_params=pltpu.CompilerParams(vmem_limit_bytes=64 * 1024 * 1024 - 128 * 1024),
    )(right_side, factor_window.T, diag_inverse)

    def device(row, col):
        return row * col_count + col

    planes = [
        [device(2 * turn + low_bit, 2 * j + core) for low_bit in range(2) for j in range(blocks)]
        for turn in range(turns)
        for core in range(2)
    ]
    copies, cov = lax.optimization_barrier((copies, phase_cov))
    plane = lax.all_to_all(copies, ("row", "col"), 0, 0, axis_index_groups=planes, tiled=True)
    cores = [(col, col ^ 1) for col in range(col_count)]
    cut_shapes = [jax.ShapeDtypeStruct((count, col_width, TILE_ROWS), jnp.float32) for count in (blocks, *CORE_PARTS)]
    keep, *gives = pl.pallas_call(
        cut_tiles,
        out_shape=cut_shapes,
        in_specs=[vmem],
        out_specs=[vmem] * len(cut_shapes),
        compiler_params=params,
    )(cov)
    cut = pl.pallas_call(
        pair_rows,
        out_shape=jax.ShapeDtypeStruct((blocks, 2 * col_width, TILE_ROWS), jnp.float32),
        in_specs=[vmem] * len(cut_shapes),
        out_specs=vmem,
        compiler_params=params,
    )(keep, *[lax.ppermute(give, "col", cores) for give in gives])
    beside = lax.ppermute(side, "row", [(row, row ^ 1) for row in range(row_count)])
    plane, cut, beside = lax.optimization_barrier((plane, cut, beside))
    excess = pl.pallas_call(
        pick_excess,
        out_shape=jax.ShapeDtypeStruct((PLANE_BLOCKS - 1, col_width, block_rows), jnp.float32),
        in_specs=[vmem],
        out_specs=vmem,
        compiler_params=params,
    )(plane)
    excess, cut = lax.optimization_barrier((excess, cut))
    groups = [[2 * j + core for j in range(blocks)] for core in range(2)]
    phase = lax.all_to_all(cut, "col", 0, 0, axis_index_groups=groups, tiled=True).reshape(col_count * col_width, TILE_ROWS)
    got = lax.ppermute(excess, "row", [(row, 2 * (turns - 1 - row // 2) + row % 2) for row in range(row_count)])
    plane = pl.pallas_call(
        even_out,
        out_shape=jax.ShapeDtypeStruct(((PLANE_BLOCKS + 2) * col_width, block_rows), jnp.float32),
        in_specs=[vmem] * 4,
        out_specs=vmem,
        compiler_params=params,
    )(plane, got, side, beside)
    slots = [plane]
    for step in range(1, turns):
        turn_on = [(2 * turn + bit, 2 * ((turn + step) % turns) + bit) for turn in range(turns) for bit in range(2)]
        slots.append(lax.ppermute(plane, "row", turn_on))
    own = jnp.stack(slots)
    other = lax.ppermute(own, "col", cores)
    low, solved = pl.pallas_call(
        block_solve,
        out_shape=[
            jax.ShapeDtypeStruct((rank_width, row_count * block_rows), jnp.bfloat16),
            jax.ShapeDtypeStruct((col_width, rank_width), jnp.float32),
        ],
        in_specs=[vmem, vmem],
        out_specs=[vmem, vmem],
        scratch_shapes=[
            pltpu.VMEM((row_count, rank_width, block_rows), jnp.float32),
            pltpu.VMEM((rank_width, block_rows), jnp.float32),
        ],
        compiler_params=params,
        cost_estimate=pl.CostEstimate(flops=1_600_000_000, bytes_accessed=3_000_000, transcendentals=0),
    )(own, other)
    basis = pl.pallas_call(
        tile_basis,
        out_shape=jax.ShapeDtypeStruct((TILE_ROWS, rank_width), jnp.float32),
        in_specs=[vmem, vmem],
        out_specs=vmem,
        scratch_shapes=[pltpu.VMEM((rank_width, rank_width), jnp.float32)],
        compiler_params=params,
        cost_estimate=pl.CostEstimate(flops=1_000_000_000, bytes_accessed=3_000_000, transcendentals=0),
    )(low, phase)
    basis = basis.reshape(col_count, TILE_ROWS // col_count, rank_width)
    return (lax.all_to_all(basis, "col", 0, 0, tiled=True), solved)


def solution(mesh):
    in_specs = (P("row", None), P("row", "col"), P("row", None), P("col", "row"))
    out_specs = (P("row", "col", None), P("col", None))
    return jax.shard_map(local, mesh=mesh, in_specs=in_specs, out_specs=out_specs, check_vma=False)
```

```python
import functools

import jax
import jax.numpy as jnp
from jax import lax
from jax.experimental import pallas as pl
from jax.experimental.pallas import tpu as pltpu
from jax.sharding import PartitionSpec as P

TILE_ROWS = 512
PANEL = 64
SUBLANES = 8
TURNS = 4
PLANE_BLOCKS = 7
CORE_PARTS = (3, 3, 2)
HIGHEST = lax.Precision.HIGHEST
VMEM_BYTES = 48 * 1024 * 1024


def contract(a, b, da, db):
    return lax.dot_general(a, b, (((da,), (db,)), ((), ())), precision=HIGHEST, preferred_element_type=jnp.float32)


def split(a):
    high = a.astype(jnp.bfloat16)
    return high, (a - high.astype(jnp.float32)).astype(jnp.bfloat16)


def dot3(a, b):
    dot = functools.partial(jnp.dot, preferred_element_type=jnp.float32)
    return dot(a[0], b[0]) + (dot(a[0], b[1]) + dot(a[1], b[0]))


def place_of(block_row, block_col):
    turn = block_row // 2
    count = block_col + block_row % 2 * 2 * turn
    if count < PLANE_BLOCKS:
        return turn, count
    return TURNS - 1 - turn, count - PLANE_BLOCKS + 4 * (TURNS - 1 - turn) + 1


def prepare(right_hbm, factor_hbm, diag_hbm, copies_ref, side_ref, right, factor, diag, scratch, arrived):
    sources = ((diag_hbm, diag), (factor_hbm, factor), (right_hbm, right))
    copies = [pltpu.make_async_copy(source, target, arrived.at[i]) for i, (source, target) in enumerate(sources)]
    for copy in copies:
        copy.start()
    for copy in copies:
        copy.wait()
    scaled = contract(factor[...], diag[...], 1, 1)
    for at in range(copies_ref.shape[0]):
        copies_ref[at] = scaled
    scratch[...] = contract(right[...], diag[...], 0, 1)
    half = side_ref.shape[0]
    side_ref[...] = scratch[pl.ds(pl.multiple_of(lax.axis_index("col") % 2 * half, half), half), :]


def plane_index(turn, count, last):
    return jnp.minimum(jnp.where(count < 2 * turn, count, count + (last + 1) // 2 - 2 * turn), last)


def pick_excess(plane_ref, send_ref):
    turn = lax.axis_index("row") // 2
    for at in range(send_ref.shape[0]):
        send_ref[at] = plane_ref[plane_index(turn, at + PLANE_BLOCKS, plane_ref.shape[0] - 1)]


def even_out(plane_ref, got_ref, side_ref, beside_ref, out_ref):
    row = lax.axis_index("row")
    turn = row // 2
    places, half, _ = plane_ref.shape
    for at in range(PLANE_BLOCKS):
        held = (turn >= TURNS // 2) | (at <= 4 * turn)
        other = jnp.clip(at - 4 * turn - 1, 0, got_ref.shape[0] - 1)
        own = plane_ref[plane_index(turn, at, places - 1)]
        out_ref[at * half : (at + 1) * half] = jnp.where(held, own, got_ref[other])
    for low_bit in range(2):
        start = (PLANE_BLOCKS + low_bit) * half
        out_ref[start : start + half] = jnp.where(row % 2 == low_bit, side_ref[...], beside_ref[...])


def factor_and_invert(work, size):
    shape = (SUBLANES, size)
    lane = lax.broadcasted_iota(jnp.int32, shape, 1)
    sublane = lax.broadcasted_iota(jnp.int32, shape, 0)
    for start in range(0, size, PANEL):
        end = start + PANEL
        groups = [work[at : at + SUBLANES, :] for at in range(start, end, SUBLANES)]
        for g in range(len(groups)):
            first = start + g * SUBLANES
            inside = (lane >= first) & (lane < first + SUBLANES)
            columns = [jnp.broadcast_to(groups[g][:, first + j : first + j + 1], shape) for j in range(SUBLANES)]
            pivot = {(i, j): jnp.broadcast_to(columns[j][i : i + 1, :], shape) for j in range(SUBLANES) for i in range(j, SUBLANES)}
            rows, scales = [], []
            for i in range(SUBLANES):
                row = jnp.broadcast_to(groups[g][i : i + 1, :], shape)
                rows.append(jnp.where(inside, jnp.where(lane == first + i, 1.0, 0.0), row))
            for j in range(SUBLANES):
                scale = lax.rsqrt(pivot[j, j])
                scales.append(scale)
                rows[j] = rows[j] * scale
                for i in range(j + 1, SUBLANES):
                    pivot[i, j] = pivot[i, j] * scale
                for i in range(j + 1, SUBLANES):
                    for k in range(j + 1, i + 1):
                        pivot[i, k] = pivot[i, k] - pivot[i, j] * pivot[k, j]
                    rows[i] = rows[i] - pivot[i, j] * rows[j]
            merged = rows[0]
            for i in range(1, SUBLANES):
                merged = jnp.where(sublane == i, rows[i], merged)
            groups[g] = merged
            for h in range(g + 1, len(groups)):
                left = []
                rest = jnp.where(inside, 0.0, groups[h])
                for j in range(SUBLANES):
                    column = jnp.broadcast_to(groups[h][:, first + j : first + j + 1], shape)
                    for i in range(j):
                        column = column - left[i] * pivot[j, i]
                    left.append(column * scales[j])
                    rest = rest - left[j] * rows[j]
                groups[h] = rest
        panel = jnp.concatenate(groups, axis=0)
        work[start:end, :] = panel
        if end < size:
            row_lane = lax.broadcasted_iota(jnp.int32, (size - end, size), 1)
            rest = jnp.where((row_lane >= start) & (row_lane < end), 0.0, work[end:, :])
            panel_lane = lax.broadcasted_iota(jnp.int32, panel.shape, 1)
            panel_row = lax.broadcasted_iota(jnp.int32, panel.shape, 0) + start
            known = jnp.where((panel_lane <= panel_row) | (panel_lane >= end), panel, 0.0)
            work[end:, :] = rest - contract(panel, known, 0, 0)[end:, :]
    square = (size, size)
    lower = lax.broadcasted_iota(jnp.int32, square, 1) <= lax.broadcasted_iota(jnp.int32, square, 0)
    work[...] = jnp.where(lower, work[...], 0.0)


def cut_tiles(cov_ref, keep_ref, *give_refs):
    count, _, width = keep_ref.shape
    core = lax.axis_index("col") % 2
    for at in range(count):
        part = give_refs[0].shape[0]
        for out_ref, place, there in ((keep_ref, at, core), (give_refs[at // part], at % part, 1 - core)):
            tile = 2 * at + there
            out_ref[place] = cov_ref[:, pl.ds(pl.multiple_of(tile * width, width), width)].astype(jnp.float32)


def pair_rows(keep_ref, *refs):
    rows = keep_ref.shape[1]
    first = lax.axis_index("col") % 2 == 0
    got_refs, out_ref = refs[:-1], refs[-1]
    part = got_refs[0].shape[0]
    for at in range(keep_ref.shape[0]):
        keep, got = keep_ref[at], got_refs[at // part][at % part]
        out_ref[at, :rows] = jnp.where(first, keep, got)
        out_ref[at, rows:] = jnp.where(first, got, keep)


def block_solve(own_ref, other_ref, low_ref, solved_ref, solved_t, work):
    turns, _, size = own_ref.shape
    blocks = solved_t.shape[0]
    half_rows = size // 2
    col, row = lax.axis_index("col"), lax.axis_index("row")
    core = col % 2

    def rows_of(turn, half, start, count):
        slot = jnp.bitwise_xor(row // 2, turn)
        own, other = own_ref[slot, start : start + count, :], other_ref[slot, start : start + count, :]
        return jnp.where(core == half, own, other)

    current = []
    for i in range(blocks):
        start = (PLANE_BLOCKS + i % 2) * half_rows
        parts = [rows_of(i // 2, half, start, half_rows) for half in range(2)]
        current.append(jnp.concatenate(parts, axis=0))
    for j in range(blocks):
        solved_t[j] = current[j]
        low_ref[:, j * size : (j + 1) * size] = current[j].astype(jnp.bfloat16)
        if j + 1 == blocks:
            break
        solved_pair = split(current[j])
        for i in range(j + 1, blocks):
            turn, slot = place_of(i, j)
            parts = [rows_of(turn, half, slot * half_rows, half_rows) for half in range(2)]
            current[i] = current[i] - dot3(solved_pair, split(jnp.concatenate(parts, axis=0)))
    work[...] = solved_t[col // 2].T
    solved_ref[...] = work[pl.ds(pl.multiple_of(core * half_rows, half_rows), half_rows), :]


def tile_basis(low_ref, phase_ref, basis_ref, work):
    size = low_ref.shape[0]
    phase = phase_ref[...].astype(jnp.bfloat16)
    weighted_t = jnp.dot(low_ref[...], phase, preferred_element_type=jnp.float32)
    weighted = weighted_t.T
    work[...] = contract(weighted_t, weighted_t, 1, 1)
    factor_and_invert(work, size)
    basis_ref[...] = contract(weighted, work[...], 1, 1)


def local(right_side, factor_window, diag_inverse, phase_cov):
    row_count = lax.axis_size("row")
    col_count = lax.axis_size("col")
    block_rows = right_side.shape[0]
    rank_width = right_side.shape[1]
    col_width = factor_window.shape[1]
    turns = row_count // 2
    blocks = col_count // 2
    vmem = pl.BlockSpec(memory_space=pltpu.VMEM)
    params = pltpu.CompilerParams(vmem_limit_bytes=VMEM_BYTES)
    half_rank = rank_width // 2
    copies, side = pl.pallas_call(
        prepare,
        out_shape=[
            jax.ShapeDtypeStruct((2 * blocks, col_width, block_rows), jnp.float32),
            jax.ShapeDtypeStruct((half_rank, block_rows), jnp.float32),
        ],
        in_specs=[pl.BlockSpec(memory_space=pltpu.HBM)] * 3,
        out_specs=[vmem, vmem],
        scratch_shapes=[
            pltpu.VMEM(right_side.shape, jnp.float32),
            pltpu.VMEM((col_width, block_rows), jnp.float32),
            pltpu.VMEM(diag_inverse.shape, jnp.float32),
            pltpu.VMEM((rank_width, block_rows), jnp.float32),
            pltpu.SemaphoreType.DMA((3,)),
        ],
        compiler_params=pltpu.CompilerParams(vmem_limit_bytes=64 * 1024 * 1024 - 128 * 1024),
    )(right_side, factor_window.T, diag_inverse)

    def device(row, col):
        return row * col_count + col

    planes = [
        [device(2 * turn + low_bit, 2 * j + core) for low_bit in range(2) for j in range(blocks)]
        for turn in range(turns)
        for core in range(2)
    ]
    copies, cov = lax.optimization_barrier((copies, phase_cov))
    plane = lax.all_to_all(copies, ("row", "col"), 0, 0, axis_index_groups=planes, tiled=True)
    cores = [(col, col ^ 1) for col in range(col_count)]
    cut_shapes = [jax.ShapeDtypeStruct((count, col_width, TILE_ROWS), jnp.float32) for count in (blocks, *CORE_PARTS)]
    keep, *gives = pl.pallas_call(
        cut_tiles,
        out_shape=cut_shapes,
        in_specs=[vmem],
        out_specs=[vmem] * len(cut_shapes),
        compiler_params=params,
    )(cov)
    cut = pl.pallas_call(
        pair_rows,
        out_shape=jax.ShapeDtypeStruct((blocks, 2 * col_width, TILE_ROWS), jnp.float32),
        in_specs=[vmem] * len(cut_shapes),
        out_specs=vmem,
        compiler_params=params,
    )(keep, *[lax.ppermute(give, "col", cores) for give in gives])
    beside = lax.ppermute(side, "row", [(row, row ^ 1) for row in range(row_count)])
    plane, cut, beside = lax.optimization_barrier((plane, cut, beside))
    excess = pl.pallas_call(
        pick_excess,
        out_shape=jax.ShapeDtypeStruct((PLANE_BLOCKS - 1, col_width, block_rows), jnp.float32),
        in_specs=[vmem],
        out_specs=vmem,
        compiler_params=params,
    )(plane)
    excess, cut = lax.optimization_barrier((excess, cut))
    groups = [[2 * j + core for j in range(blocks)] for core in range(2)]
    phase = lax.all_to_all(cut, "col", 0, 0, axis_index_groups=groups, tiled=True).reshape(col_count * col_width, TILE_ROWS)
    got = lax.ppermute(excess, "row", [(row, 2 * (turns - 1 - row // 2) + row % 2) for row in range(row_count)])
    plane = pl.pallas_call(
        even_out,
        out_shape=jax.ShapeDtypeStruct(((PLANE_BLOCKS + 2) * col_width, block_rows), jnp.float32),
        in_specs=[vmem] * 4,
        out_specs=vmem,
        compiler_params=params,
    )(plane, got, side, beside)
    slots = [plane]
    for step in range(1, turns):
        slots.append(lax.ppermute(plane, "row", [(row, row ^ 2 * step) for row in range(row_count)]))
    own = jnp.stack(slots)
    other = lax.ppermute(own, "col", cores)
    low, solved = pl.pallas_call(
        block_solve,
        out_shape=[
            jax.ShapeDtypeStruct((rank_width, row_count * block_rows), jnp.bfloat16),
            jax.ShapeDtypeStruct((col_width, rank_width), jnp.float32),
        ],
        in_specs=[vmem, vmem],
        out_specs=[vmem, vmem],
        scratch_shapes=[
            pltpu.VMEM((row_count, rank_width, block_rows), jnp.float32),
            pltpu.VMEM((rank_width, block_rows), jnp.float32),
        ],
        compiler_params=params,
        cost_estimate=pl.CostEstimate(flops=1_600_000_000, bytes_accessed=3_000_000, transcendentals=0),
    )(own, other)
    basis = pl.pallas_call(
        tile_basis,
        out_shape=jax.ShapeDtypeStruct((TILE_ROWS, rank_width), jnp.float32),
        in_specs=[vmem, vmem],
        out_specs=vmem,
        scratch_shapes=[pltpu.VMEM((rank_width, rank_width), jnp.float32)],
        compiler_params=params,
        cost_estimate=pl.CostEstimate(flops=1_000_000_000, bytes_accessed=3_000_000, transcendentals=0),
    )(low, phase)
    basis = basis.reshape(col_count, TILE_ROWS // col_count, rank_width)
    return (lax.all_to_all(basis, "col", 0, 0, tiled=True), solved)


def solution(mesh):
    in_specs = (P("row", None), P("row", "col"), P("row", None), P("col", "row"))
    out_specs = (P("row", "col", None), P("col", None))
    return jax.shard_map(local, mesh=mesh, in_specs=in_specs, out_specs=out_specs, check_vma=False)
```
